256 devices in a mesh: tile: 32 (over y_lo, z, core), samp: 8 (over y_hi, x).
Axes of the slice: x: 4, y: 4 (y_hi: 2, y_lo: 2; y = y_hi * 2 + y_lo), z: 8, core: 2. Of those that a mesh axis runs over, the one named last changes fastest.
Arguments:
- bathymetry: float32 [6, 512, 512], P(None, 'tile'), may hold values from 0.5 to 2
- initial_state: float32 [16, 6, 512, 512], P(None, None, 'tile'), may hold values from -6 to 6
- patterns: bfloat16 [4, 6, 512, 512], P(None, None, 'tile'), may hold values from -6 to 6
- pattern_index: int32 [8, 16], P('samp'), may hold values from 0 to 3
- coupling: float32 [16, 16], replicated, may hold values from -1.5 to 1.5
- final_weights: float32 [8, 16, 6, 512, 512], P('samp', None, None, 'tile'), may hold values from -6 to 6
Outputs:
- gradient: float32 [6, 512, 512], P(None, 'tile')
The draws below stay inside these ranges and needn't reach their ends.
All inputs are finite; a program needn't handle non-finite values.
Results may differ from the reference program's by a relative error of at most 0.0003.
Values sent between devices are 32-bit elements; how exact they have to be, the bound alone decides.
A program may use at most 128 MiB of HBM per device.

```python
import math
import jax
import jax.numpy as jnp
from jax import lax

N = 512
LAYERS = 16
PATTERNS = 4
SAMPLES = 8


def set_ends(values, key, least, largest):
    place = [jax.random.randint(jax.random.fold_in(key, axis), (), 0, length) for axis, length in enumerate(values.shape)]
    main_axis = values.shape.index(max(values.shape))
    beside = place[:main_axis] + [(place[main_axis] + 1) % values.shape[main_axis]] + place[main_axis + 1:]
    return values.at[tuple(place)].set(least).at[tuple(beside)].set(largest)


def levels(stream_key, dims, cuts, low, top_value):
    level, own = 1.0, jax.random.fold_in(stream_key, 6)
    for axis_at, parts in cuts:
        heights = jnp.exp(jax.random.uniform(jax.random.fold_in(own, axis_at), (parts,), jnp.float32, low / len(cuts), top_value / len(cuts)))
        level = level * jnp.repeat(heights, dims[axis_at] // parts).reshape([-1 if axis == axis_at else 1 for axis in range(len(dims))])
    return level


def normal_values(own_key, shape, width, reach, shards=(), kind=jnp.bfloat16):
    entries = width * jax.random.normal(own_key, shape, jnp.float32)
    if shards:
        entries = entries * levels(own_key, shape, shards, -0.22, 0.18)
    return jnp.clip(entries, -reach, reach).astype(kind)


def setup_inputs(seed: int = 0) -> dict:
    key_of = jax.random.split(jax.random.key(seed), 7)
    bathymetry = jnp.clip(jnp.exp(math.log(2.0) - 1.3862944 * jax.random.uniform(key_of[0], (6, N, N), jnp.float32) ** levels(key_of[0], (6, N, N), ((1, 32),), -0.2, 0.2)), 0.5, 2.0)
    initial_state = normal_values(key_of[1], (LAYERS, 6, N, N), 1.0, 6.0, ((2, 32),), jnp.float32)
    patterns = normal_values(key_of[2], (PATTERNS, 6, N, N), 1.0, 6.0, ((2, 32),))
    pattern_index = set_ends(jax.random.randint(key_of[3], (SAMPLES, LAYERS), 0, PATTERNS), jax.random.fold_in(key_of[3], 1), 0, PATTERNS - 1).astype(jnp.int32)
    coupling = normal_values(key_of[4], (LAYERS, LAYERS), LAYERS ** -0.5, 1.5, (), jnp.float32)
    final_weights = normal_values(key_of[5], (SAMPLES, LAYERS, 6, N, N), 1.0, 6.0, ((0, 8), (3, 32)), jnp.float32)
    return dict(bathymetry=bathymetry, initial_state=initial_state, patterns=patterns, pattern_index=pattern_index, coupling=coupling, final_weights=final_weights)


STEP_FACTOR = 0.1

def pad_cube(field):
    cells = field.shape[-1]
    last = cells - 1
    padded = jnp.zeros(field.shape[:-3] + (6, cells + 2, cells + 2), field.dtype)
    padded = padded.at[..., 1:-1, 1:-1].set(field)
    western = jnp.stack([field[..., 3, last, :], field[..., 0, last, :], field[..., 1, last, :], field[..., 2, last, :], field[..., 3, ::-1, last], field[..., 3, :, 0]], axis=-2)
    eastern = jnp.stack([field[..., 1, 0, :], field[..., 2, 0, :], field[..., 3, 0, :], field[..., 0, 0, :], field[..., 1, :, last], field[..., 1, ::-1, 0]], axis=-2)
    southern = jnp.stack([field[..., 5, :, last], field[..., 5, last, ::-1], field[..., 5, ::-1, 0], field[..., 5, 0, :], field[..., 0, :, last], field[..., 2, ::-1, 0]], axis=-2)
    northern = jnp.stack([field[..., 4, :, 0], field[..., 4, last, :], field[..., 4, ::-1, last], field[..., 4, 0, ::-1], field[..., 2, ::-1, last], field[..., 0, :, 0]], axis=-2)
    padded = padded.at[..., :, 0, 1:-1].set(western)
    padded = padded.at[..., :, -1, 1:-1].set(eastern)
    padded = padded.at[..., :, 1:-1, 0].set(southern)
    padded = padded.at[..., :, 1:-1, -1].set(northern)
    return padded

def stencil(padded, depth_pad):
    rows_i = padded.shape[-2] - 2
    rows_j = padded.shape[-1] - 2
    centre = padded[..., 1:1 + rows_i, 1:1 + rows_j]
    depth_here = depth_pad[..., 1:1 + rows_i, 1:1 + rows_j]
    summed = jnp.zeros_like(centre)
    for shift_i, shift_j in ((1, 0), (-1, 0), (0, 1), (0, -1)):
        beside_value = padded[..., 1 + shift_i:1 + shift_i + rows_i, 1 + shift_j:1 + shift_j + rows_j]
        depth_near = depth_pad[..., 1 + shift_i:1 + shift_i + rows_i, 1 + shift_j:1 + shift_j + rows_j]
        summed = summed + 0.5 * (depth_here + depth_near) * (beside_value - centre)
    return summed

def mix_layers(matrix, state):
    return jnp.einsum('km,mpij->kpij', matrix, state, precision=lax.Precision.HIGHEST)

def reference(bathymetry, initial_state, patterns, pattern_index, coupling, final_weights):
    mixing = jnp.eye(LAYERS, dtype=coupling.dtype) + coupling

    def sample_loss(bathy, forcing, cotangent):
        depth_pad = pad_cube(bathy)
        mixed_zero = mix_layers(mixing, initial_state)
        state_one = initial_state + STEP_FACTOR * (stencil(pad_cube(mixed_zero), depth_pad) + forcing)
        mixed_one = mix_layers(mixing, state_one)
        state_two = 2.0 * state_one - initial_state + STEP_FACTOR * (stencil(pad_cube(mixed_one), depth_pad) + forcing)
        return jnp.sum(cotangent * state_two)

    def one_sample(summed, sample):
        forcing = patterns[pattern_index[sample]].astype(initial_state.dtype)
        gradient = jax.grad(sample_loss)(bathymetry, forcing, final_weights[sample])
        return (summed + gradient, None)
    summed, _ = lax.scan(one_sample, jnp.zeros_like(bathymetry), jnp.arange(SAMPLES, dtype=jnp.int32))
    return summed / SAMPLES
```

```python
import jax
import jax.numpy as jnp
from jax import lax
from jax.experimental import pallas as pl
from jax.experimental.pallas import tpu as pltpu
from jax.sharding import PartitionSpec as P

F32, BF16 = jnp.float32, jnp.bfloat16
MESH = pl.DeviceIdType.MESH
TILES, SAMPS, ROWS, CELLS, LAYERS, PANELS = 32, 8, 16, 512, 16, 6
LAST = TILES - 1


def split(x):
    high = x.astype(BF16)
    return high, (x - high.astype(F32)).astype(BF16)


def iota(shape, axis):
    return lax.broadcasted_iota(jnp.int32, shape, axis)


def dot(a, b):
    return jnp.dot(a, b, preferred_element_type=F32)


def kernel(
    depth_hbm, state_hbm, pattern_hbm, index_ref, coupling_ref, weight_hbm, out_ref,
    xs, ws, ps, bs, kz, kv, kq, field, qf, acc, ocs, pk, colh, gath, scat, prow, precv,
    mirror_out, mirror_in, hub_out, gath_p, scat_p, hub_in, part, rs_in, ag, done,
    load_x, load_w, load_pb, row_send, row_recv, hub_send, gath_recv, mir_send, mir_recv,
    scat_send, scat_recv, p_send, p_recv, pm_send, pm_recv, ph_send, pgath_recv, ps_send, ps_recv,
    rs_send, rs_recv, ag_send, ag_recv,
):
    t = lax.axis_index("tile")
    s = lax.axis_index("samp")
    left, right, mirror = (t + LAST) % TILES, (t + 1) % TILES, LAST - t
    is_first, is_last = t == 0, t == LAST
    is_hub = jnp.logical_or(is_first, is_last)
    at_end = t // LAST
    at_start = mirror // LAST

    barrier = pltpu.get_barrier_semaphore()

    def greet(device):
        pl.semaphore_signal(barrier, inc=1, device_id=device, device_id_type=MESH)

    def tell_tile(u, c):
        @pl.when(u != t)
        def _():
            greet({"tile": u})
        return c

    lax.fori_loop(0, TILES, tell_tile, 0)

    def tell_samp(u, c):
        @pl.when(u != s)
        def _():
            greet({"samp": u})
        return c

    lax.fori_loop(0, SAMPS, tell_samp, 0)

    def load(p):
        return (
            pltpu.make_async_copy(state_hbm.at[:, p], xs.at[p], load_x.at[p]),
            pltpu.make_async_copy(weight_hbm.at[0, :, p], ws.at[p], load_w.at[p]),
        )

    def panel_at(step):
        return jnp.minimum(1 + 2 * step, 10 - 2 * step)

    load_p = pltpu.make_async_copy(pattern_hbm, ps, load_pb.at[0])
    load_b = pltpu.make_async_copy(depth_hbm, bs, load_pb.at[1])
    for step in range(PANELS):
        for copy in load(min(1 + 2 * step, 10 - 2 * step)):
            copy.start()
        if step == 0:
            load_p.start()
            load_b.start()

    mixing = coupling_ref[...] + jnp.where(iota((16, 16), 0) == iota((16, 16), 1), 1.0, 0.0)
    to_layer = (iota((256, 16), 0) % 16 == iota((256, 16), 1)).astype(BF16)
    from_layer = (iota((16, 256), 0) == iota((16, 256), 1) // 16).astype(BF16)
    same_row = iota((256, 256), 0) // 16 == iota((256, 256), 1) % 16

    def spread(matrix):
        tall = dot(to_layer, matrix).astype(BF16)
        return jnp.where(same_row, dot(tall, from_layer), 0.0).astype(BF16)

    for target, matrix in ((kz, mixing), (kv, mixing.T)):
        high, low = split(matrix)
        spread_high = spread(high)
        target[:, 0:256] = spread_high
        target[:, 256:512] = spread(low)
        target[:, 512:768] = spread_high
    thirty = jnp.where(
        jnp.logical_and(same_row, iota((256, 256), 0) % 16 == iota((256, 256), 1) // 16), 30.0, 0.0
    ).astype(BF16)
    kq[:, 0:256] = thirty
    kq[:, 256:512] = thirty
    chosen = (iota((4, 16), 0) == jnp.broadcast_to(index_ref[...], (4, 16))).astype(F32)
    tall = lax.dot_general(
        to_layer, chosen.astype(BF16), (((1,), (1,)), ((), ())), preferred_element_type=F32
    ).astype(BF16)
    from_pattern = (iota((4, 64), 0) == iota((4, 64), 1) // 16).astype(BF16)
    kq[:, 512:576] = jnp.where(
        iota((256, 64), 0) // 16 == iota((256, 64), 1) % 16, dot(tall, from_pattern), 0.0
    ).astype(BF16)

    acc[...] = jnp.zeros_like(acc)
    lanes = iota((8, 128), 1)
    pl.semaphore_wait(barrier, TILES - 1 + SAMPS - 1)

    def remote(src, dst, send, recv, device):
        return pltpu.make_async_remote_copy(
            src_ref=src, dst_ref=dst, send_sem=send, recv_sem=recv,
            device_id=device, device_id_type=MESH,
        )

    def row_south(p):
        to = p + jnp.where(p < 4, at_end * ((p + 1) % 4 - p), 0)
        return remote(field.at[p, 16], field.at[to, 0], row_send.at[0, p], row_recv.at[0, to], {"tile": right})

    def row_north(p):
        to = p + jnp.where(p < 4, at_start * ((p + 3) % 4 - p), 0)
        return remote(field.at[p, 1], field.at[to, 17], row_send.at[1, p], row_recv.at[1, to], {"tile": left})

    def came_from_left(p):
        return remote(field.at[p, 16], field.at[p, 0], row_send.at[0, p], row_recv.at[0, p], {"tile": right})

    def came_from_right(p):
        return remote(field.at[p, 1], field.at[p, 17], row_send.at[1, p], row_recv.at[1, p], {"tile": left})

    def south_goes(p):
        return jnp.logical_or(p < 4, jnp.logical_not(is_last))

    def north_goes(p):
        return jnp.logical_or(p < 4, jnp.logical_not(is_first))

    def gather_to(hub):
        panel = 1 if hub else 3
        return remote(pk.at[panel], gath.at[t], hub_send.at[panel // 2], gath_recv.at[t], {"tile": hub})

    MIRRORED = (((2, 0), (5, 0)), ((2, 1), (4, 1)), ((5, 0), (2, 0)), ((4, 1), (2, 1)))

    def mirrored(n):
        (a, b), (c, d) = MIRRORED[n]
        return remote(pk.at[a, b], colh.at[c, d], mir_send.at[n], mir_recv.at[n], {"tile": mirror})

    def scatter_to(u, panel):
        return remote(scat.at[u], colh.at[panel], scat_send.at[u], scat_recv.at[panel // 2], {"tile": u})

    def seg_w(u):
        return jnp.where(is_last, LAST - u, u)

    def seg_e(u):
        return jnp.where(is_last, u, LAST - u)

    def make_scatter():
        slot = jnp.where(is_last, 16, 1)

        def one(u, c):
            for side in range(2):
                seg = seg_e(u) if side else seg_w(u)
                block, place = seg // 8, seg % 8
                out = jnp.zeros((8, 128), F32)
                for g in range(5):
                    x = field[5 - side, slot, pl.ds(8 * g, 8), pl.ds(pl.multiple_of(block * 128, 128), 128)]
                    x = pltpu.roll(x, (16 * g - 16 * place + 128) % 128, 1)
                    out = jnp.where(lanes // 16 == g, x, out)
                scat[u, side] = out

            @pl.when(jnp.logical_and(u != t, is_last))
            def _():
                scatter_to(u, 1).start()

            @pl.when(jnp.logical_and(u != t, is_first))
            def _():
                scatter_to(u, 3).start()

            return c

        lax.fori_loop(0, TILES, one, 0)

        @pl.when(is_last)
        def _():
            colh[1] = scat[t]

        @pl.when(is_first)
        def _():
            colh[3] = scat[t]

    def mix(step, c):
        p = panel_at(step)
        for copy in load(p):
            copy.wait()
        xh, xl = split(xs[p].reshape(256, CELLS))
        z = dot(kz[...], jnp.concatenate([xh, xh, xl], 0))
        field[p, 1:17, 0:16, :] = z.reshape(ROWS, 16, CELLS)
        pat = ps[:, p].reshape(64, CELLS)
        q = dot(kq[...], jnp.concatenate([xh, xl, pat], 0))
        qf[p] = q.reshape(ROWS, 16, CELLS)
        wh, wl = split(ws[p].reshape(256, CELLS))
        v = dot(kv[...], jnp.concatenate([wh, wh, wl], 0))
        field[p, 1:17, 16:32, :] = v.reshape(ROWS, 16, CELLS)
        for i in range(ROWS):
            field[p, 1 + i, 32:40, :] = jnp.broadcast_to(0.5 * bs[p, i : i + 1, :], (8, CELLS))

        @pl.when(south_goes(p))
        def _():
            row_south(p).start()

        @pl.when(north_goes(p))
        def _():
            row_north(p).start()

        for side in range(2):
            if side == 0:
                rev = jnp.where(jnp.logical_or(p == 1, jnp.logical_or(p == 2, p == 5)), 1, 0)
            else:
                rev = jnp.where(jnp.logical_and(p >= 2, p <= 4), 1, 0)
            out = jnp.zeros((8, 128), F32)
            for i in range(ROWS):
                for g in range(5):
                    if side == 0:
                        x = field[p, 1 + i, 8 * g : 8 * g + 8, 0:128][:, 0:1]
                    else:
                        x = field[p, 1 + i, 8 * g : 8 * g + 8, CELLS - 128 : CELLS][:, 127:128]
                    spot = 16 * g + i + rev * (15 - 2 * i)
                    out = jnp.where(lanes == spot, jnp.broadcast_to(x, (8, 128)), out)
            pk[p, side] = out

        for at, hub in ((0, LAST), (1, 0)):
            @pl.when(jnp.logical_and(step == at, t != hub))
            def _():
                gather_to(hub).start()

            @pl.when(jnp.logical_and(step == at, t == hub))
            def _():
                gath[t] = pk[1 if hub else 3]

        @pl.when(jnp.logical_and(step == 3, is_hub))
        def _():
            make_scatter()

        return c

    load_p.wait()
    load_b.wait()
    lax.fori_loop(0, PANELS, mix, 0)

    for n in range(4):
        mirrored(n).start()
    colh[0, 0] = pk[5, 1]
    colh[0, 1] = pk[4, 0]
    colh[4, 0] = pk[0, 1]
    colh[5, 1] = pk[0, 0]

    first_lane, last_lane = lanes == 0, lanes == 127

    def blocks(x):
        return [x[:, 128 * k : 128 * k + 128] for k in range(4)]

    def to_left(b, tail):
        r = [pltpu.roll(x, 127, 1) for x in b] + [tail]
        return [jnp.where(last_lane, r[k + 1], r[k]) for k in range(4)]

    def to_right(b, head):
        r = [head] + [pltpu.roll(x, 1, 1) for x in b]
        return [jnp.where(first_lane, r[k], r[k + 1]) for k in range(4)]

    def add(a, b):
        return [x + y for x, y in zip(a, b)]

    def sub(a, b):
        return [x - y for x, y in zip(a, b)]

    def mul(a, b):
        return [x * y for x, y in zip(a, b)]

    def stencil_row(p, i):
        slot = i + 1
        west, east = colh[p, 0], colh[p, 1]
        rev_w, rev_e = jnp.where(p == 1, 1, 0), jnp.where(p == 3, 1, 0)
        lane_w = i + rev_w * (15 - 2 * i)
        lane_e = i + rev_e * (15 - 2 * i)

        def rows(g, at):
            return blocks(field[p, at, 8 * g : 8 * g + 8, :])

        def from_west(g):
            return pltpu.roll(west, (128 - 16 * g - lane_w) % 128, 1)

        def from_east(g):
            return pltpu.roll(east, (127 - 16 * g - lane_e) % 128, 1)

        h = rows(4, slot)
        beta_e = add(h, to_left(h, from_east(4)))
        beta_w = to_right(beta_e, h[0] + from_west(4))
        beta_s = add(h, rows(4, slot + 1))
        beta_n = add(h, rows(4, slot - 1))

        def lap(g):
            x = rows(g, slot)
            de = sub(to_left(x, from_east(g)), x)
            dw = to_right(de, x[0] - from_west(g))
            ds = sub(rows(g, slot + 1), x)
            dn = sub(x, rows(g, slot - 1))
            total = sub(add(mul(beta_e, de), mul(beta_s, ds)), add(mul(beta_w, dw), mul(beta_n, dn)))
            return total, de, dw, ds, dn

        sums = None
        for half in range(2):
            lz, *dz = lap(half)
            lv, *dv = lap(2 + half)
            q = add(lz, blocks(qf[p, i, 8 * half : 8 * half + 8, :]))
            terms = [add(mul(a, q), mul(b, lv)) for a, b in zip(dv, dz)]
            sums = terms if sums is None else [add(a, b) for a, b in zip(sums, terms)]
        pe, pw, ps_, pn = sums
        zero = jnp.zeros((8, 128), F32)
        own = sub(add(pe, ps_), add(pw, pn))
        move_e = to_right(pe, zero)
        move_w = to_left(pw, zero)
        own = add(own, sub(move_e, move_w))
        ocs[p, i] = jnp.where(
            first_lane, pltpu.roll(pe[3], 1, 1), jnp.where(last_lane, -pltpu.roll(pw[0], 127, 1), 0.0)
        )
        return [-x for x in pn], own, ps_

    def accumulate(p, slot, value):
        for k in range(4):
            acc[p, slot, :, 128 * k : 128 * k + 128] += value[k]

    def stencil_rows(p, start, count):
        pending = {}
        for r in range(count):
            for offset, value in enumerate(stencil_row(p, start + r)):
                key = r + offset
                pending[key] = add(pending[key], value) if key in pending else value
            accumulate(p, start + r, pending.pop(r))
        for key, value in pending.items():
            accumulate(p, start + key, value)

    def wait_columns():
        for n in range(4):
            mirrored(n).wait_recv()

        @pl.when(t != LAST)
        def _():
            scatter_to(LAST, 1).wait_recv()

        @pl.when(t != 0)
        def _():
            scatter_to(0, 3).wait_recv()

    def inner(p, c):
        @pl.when(p == 1)
        def _():
            wait_columns()

        def two(n, c):
            stencil_rows(p, 1 + 2 * n, 2)
            return c

        lax.fori_loop(0, 7, two, 0)
        return c

    lax.fori_loop(0, PANELS, inner, 0)

    @pl.when(is_hub)
    def _():
        def wait_one(u, c):
            @pl.when(u != t)
            def _():
                remote(pk.at[1], gath.at[u], hub_send.at[0], gath_recv.at[u], {"tile": u}).wait_recv()
            return c

        lax.fori_loop(0, TILES, wait_one, 0)
        slot = jnp.where(is_last, 17, 0)

        def one(block, c):
            for side in range(2):
                for g in range(5):
                    out = jnp.zeros((8, 128), F32)
                    for k in range(8):
                        seg = 8 * block + k
                        u = seg_e(seg) if side else seg_w(seg)
                        x = pltpu.roll(gath[u, side], (16 * k - 16 * g + 128) % 128, 1)
                        out = jnp.where(lanes // 16 == k, x, out)
                    field[5 - side, slot, pl.ds(8 * g, 8), pl.ds(pl.multiple_of(block * 128, 128), 128)] = out
            return c

        lax.fori_loop(0, 4, one, 0)

    def outer(p, c):
        @pl.when(jnp.logical_or(p < 4, jnp.logical_not(is_first)))
        def _():
            came_from_left(p).wait_recv()

        @pl.when(jnp.logical_or(p < 4, jnp.logical_not(is_last)))
        def _():
            came_from_right(p).wait_recv()

        stencil_rows(p, 0, 1)
        stencil_rows(p, ROWS - 1, 1)
        return c

    lax.fori_loop(0, PANELS, outer, 0)

    def fold(matrix, x):
        high, low = split(x)
        return dot(matrix, high) + dot(matrix, low)

    fold_rows = (iota((ROWS, 8 * ROWS), 0) == iota((ROWS, 8 * ROWS), 1) // 8).astype(BF16)
    fold_panels = (iota((8, 8 * PANELS), 0) == iota((8, 8 * PANELS), 1) // 8).astype(BF16)
    prow[0] = fold(fold_panels, acc[:, 0].reshape(8 * PANELS, CELLS))
    prow[1] = fold(fold_panels, acc[:, 17].reshape(8 * PANELS, CELLS))
    p_south = remote(prow.at[1], precv.at[0], p_send.at[0], p_recv.at[0], {"tile": right})
    p_north = remote(prow.at[0], precv.at[1], p_send.at[1], p_recv.at[1], {"tile": left})
    p_south.start()
    p_north.start()

    lane16, row16 = iota((16, 128), 1), iota((16, 128), 0)
    leaving = [fold(fold_rows, ocs[p].reshape(8 * ROWS, 128)) for p in range(PANELS)]

    def leaving_column(p, side):
        return leaving[p][:, 0:1] if side else leaving[p][:, 127:128]

    def leaving_row(p, side, reverse):
        spot = 15 - row16 if reverse else row16
        column = jnp.broadcast_to(leaving_column(p, side), (16, 128))
        return jnp.sum(jnp.where(lane16 == spot, column, 0.0), axis=0, keepdims=True)

    mirror_out[...] = jnp.zeros_like(mirror_out)
    for n in range(4):
        (a, b), _ = MIRRORED[n]
        mirror_out[n : n + 1, :] = leaving_row(a, b, True)
    p_mirror = remote(mirror_out, mirror_in, pm_send.at[0], pm_recv.at[0], {"tile": mirror})
    p_mirror.start()

    def gather_p(hub):
        n = 0 if hub else 1
        return remote(hub_out.at[n], gath_p.at[t], ph_send.at[n], pgath_recv.at[t], {"tile": hub})

    up, down = t % 8, (LAST - t) % 8
    for n, hub in enumerate((LAST, 0)):
        panel = 1 if hub else 3
        hub_out[n] = jnp.zeros((8, 128), F32)
        hub_out[n, 0:1, :] = pltpu.roll(leaving_row(panel, 0, bool(hub)), 16 * (down if hub else up), 1)
        hub_out[n, 1:2, :] = pltpu.roll(leaving_row(panel, 1, not hub), 16 * (up if hub else down), 1)

        @pl.when(t != hub)
        def _():
            gather_p(hub).start()

        @pl.when(t == hub)
        def _():
            gath_p[t] = hub_out[n]

    def scatter_p(u, hub):
        n = 0 if hub else 1
        return remote(scat_p.at[u // 8], hub_in.at[n], ps_send.at[u], ps_recv.at[n], {"tile": u})

    @pl.when(is_hub)
    def _():
        rows = prow[jnp.where(is_last, 1, 0)]
        for block in range(4):
            ahead = rows[:, 128 * block : 128 * block + 128]
            behind = rows[:, 128 * (3 - block) : 128 * (3 - block) + 128]
            w = jnp.where(is_last, behind, ahead)
            e = jnp.where(is_last, ahead, behind)
            scat_p[block] = jnp.zeros((8, 128), F32)
            scat_p[block, 0:1, :] = w[5:6]
            scat_p[block, 1:2, :] = e[4:5]

        def one(u, c):
            @pl.when(jnp.logical_and(u != t, is_last))
            def _():
                scatter_p(u, LAST).start()

            @pl.when(jnp.logical_and(u != t, is_first))
            def _():
                scatter_p(u, 0).start()

            return c

        lax.fori_loop(0, TILES, one, 0)

        @pl.when(is_last)
        def _():
            hub_in[0] = scat_p[t // 8]

        @pl.when(is_first)
        def _():
            hub_in[1] = scat_p[t // 8]

    for p in range(PANELS):
        part[p] = fold(fold_rows, acc[p, 1:17].reshape(8 * ROWS, CELLS))

    def add_column(p, side, column):
        if side:
            at, lane = CELLS - 128, 127
        else:
            at, lane = 0, 0
        spread_out = jnp.broadcast_to(column, (16, 128))
        part[p, :, at : at + 128] += jnp.where(lane16 == lane, spread_out, 0.0)

    add_column(5, 1, leaving_column(0, 0))
    add_column(4, 0, leaving_column(0, 1))
    add_column(0, 1, leaving_column(4, 0))
    add_column(0, 0, leaving_column(5, 1))

    def row_to_column(row, base, reverse):
        spot = base + (15 - row16 if reverse else row16)
        spread_out = jnp.broadcast_to(row, (16, 128))
        return jnp.sum(jnp.where(lane16 == spot, spread_out, 0.0), axis=1, keepdims=True)

    p_south.wait_recv()
    p_north.wait_recv()
    panel_row = iota((8, CELLS), 0)
    from_north = precv[0]
    from_south = precv[1]
    pad = jnp.zeros((4, CELLS), F32)
    from_north = jnp.where(is_first, jnp.concatenate([from_north[3:4], from_north[0:3], pad], 0), from_north)
    from_south = jnp.where(is_last, jnp.concatenate([from_south[1:4], from_south[0:1], pad], 0), from_south)
    for p in range(PANELS):
        part[p, 0:1, :] += from_north[p : p + 1]
        part[p, ROWS - 1 : ROWS, :] += from_south[p : p + 1]

    p_mirror.wait_recv()
    for n in range(4):
        _, (a, b) = MIRRORED[n]
        add_column(a, b, row_to_column(mirror_in[n : n + 1, :], 0, False))

    @pl.when(t != LAST)
    def _():
        scatter_p(LAST, LAST).wait_recv()

    @pl.when(t != 0)
    def _():
        scatter_p(0, 0).wait_recv()

    add_column(1, 0, row_to_column(hub_in[0, 0:1, :], 16 * down, True))
    add_column(1, 1, row_to_column(hub_in[0, 1:2, :], 16 * up, False))
    add_column(3, 0, row_to_column(hub_in[1, 0:1, :], 16 * up, False))
    add_column(3, 1, row_to_column(hub_in[1, 1:2, :], 16 * down, True))

    @pl.when(is_hub)
    def _():
        def wait_one(u, c):
            @pl.when(u != t)
            def _():
                remote(hub_out.at[0], gath_p.at[u], ph_send.at[0], pgath_recv.at[u], {"tile": u}).wait_recv()
            return c

        lax.fori_loop(0, TILES, wait_one, 0)

        def hub_row(block, side):
            total = jnp.zeros((8, 128), F32)
            for k in range(8):
                seg = 8 * block + k
                total = total + gath_p[seg_e(seg) if side else seg_w(seg)]
            return total[side : side + 1, :]

        for block in range(4):
            for side in range(2):
                row = hub_row(block, side)
                at = 128 * block

                @pl.when(is_last)
                def _():
                    part[5 - side, ROWS - 1 : ROWS, at : at + 128] += row

                @pl.when(is_first)
                def _():
                    part[5 - side, 0:1, at : at + 128] += row

    for n in range(SAMPS):
        h, k = n // 4, n % 4
        rs_in[n] = part[:, 8 * h : 8 * h + 8, 128 * k : 128 * k + 128]

    def each_peer(fn):
        def one(d, c):
            fn((s + d) % SAMPS)
            return c

        lax.fori_loop(1, SAMPS, one, 0)

    def reduce_to(peer):
        return remote(rs_in.at[peer], ag.at[s], rs_send.at[peer], rs_recv.at[s], {"samp": peer})

    def reduce_from(peer):
        return remote(rs_in.at[peer], ag.at[peer], rs_send.at[peer], rs_recv.at[peer], {"samp": peer})

    each_peer(lambda peer: reduce_to(peer).start())
    ag[s] = rs_in[s]
    each_peer(lambda peer: reduce_from(peer).wait_recv())
    each_peer(lambda peer: reduce_to(peer).wait_send())
    total = ag[0]
    for n in range(1, SAMPS):
        total = total + ag[n]
    done[s] = total * (0.005 / SAMPS)

    def share_with(peer):
        return remote(done.at[s], done.at[s], ag_send.at[peer], ag_recv.at[s], {"samp": peer})

    def share_from(peer):
        return remote(done.at[peer], done.at[peer], ag_send.at[peer], ag_recv.at[peer], {"samp": peer})

    each_peer(lambda peer: share_with(peer).start())
    each_peer(lambda peer: share_from(peer).wait_recv())
    for n in range(SAMPS):
        h, k = n // 4, n % 4
        out_ref[:, 8 * h : 8 * h + 8, 128 * k : 128 * k + 128] = done[n]

    each_peer(lambda peer: share_with(peer).wait_send())
    for p in range(PANELS):
        @pl.when(south_goes(p))
        def _():
            row_south(p).wait_send()

        @pl.when(north_goes(p))
        def _():
            row_north(p).wait_send()

    for n in range(4):
        mirrored(n).wait_send()
    p_south.wait_send()
    p_north.wait_send()
    p_mirror.wait_send()
    for hub in (LAST, 0):
        @pl.when(t != hub)
        def _():
            gather_to(hub).wait_send()
            gather_p(hub).wait_send()

    @pl.when(is_hub)
    def _():
        def one(u, c):
            @pl.when(u != t)
            def _():
                scatter_to(u, 1).wait_send()
                scatter_p(u, LAST).wait_send()
            return c

        lax.fori_loop(0, TILES, one, 0)


def body(bathymetry, initial_state, patterns, pattern_index, coupling, final_weights):
    vmem = pl.BlockSpec(memory_space=pltpu.VMEM)
    hbm = pl.BlockSpec(memory_space=pl.ANY)
    tile = (8, 128)
    dma = pltpu.SemaphoreType.DMA
    return pl.pallas_call(
        kernel,
        out_shape=jax.ShapeDtypeStruct((PANELS, ROWS, CELLS), F32),
        in_specs=[hbm, hbm, hbm, vmem, vmem, hbm],
        out_specs=vmem,
        scratch_shapes=[
            pltpu.VMEM((PANELS, LAYERS, ROWS, CELLS), F32),
            pltpu.VMEM((PANELS, LAYERS, ROWS, CELLS), F32),
            pltpu.VMEM((4, PANELS, ROWS, CELLS), BF16),
            pltpu.VMEM((PANELS, ROWS, CELLS), F32),
            pltpu.VMEM((256, 768), BF16),
            pltpu.VMEM((256, 768), BF16),
            pltpu.VMEM((256, 576), BF16),
            pltpu.VMEM((PANELS, ROWS + 2, 40, CELLS), F32),
            pltpu.VMEM((PANELS, ROWS, LAYERS, CELLS), F32),
            pltpu.VMEM((PANELS, ROWS + 2, 8, CELLS), F32),
            pltpu.VMEM((PANELS, ROWS) + tile, F32),
            pltpu.VMEM((PANELS, 2) + tile, F32),
            pltpu.VMEM((PANELS, 2) + tile, F32),
            pltpu.VMEM((TILES, 2) + tile, F32),
            pltpu.VMEM((TILES, 2) + tile, F32),
            pltpu.VMEM((2, 8, CELLS), F32),
            pltpu.VMEM((2, 8, CELLS), F32),
            pltpu.VMEM(tile, F32),
            pltpu.VMEM(tile, F32),
            pltpu.VMEM((2,) + tile, F32),
            pltpu.VMEM((TILES,) + tile, F32),
            pltpu.VMEM((4,) + tile, F32),
            pltpu.VMEM((2,) + tile, F32),
            pltpu.VMEM((PANELS, ROWS, CELLS), F32),
            pltpu.VMEM((SAMPS, PANELS) + tile, F32),
            pltpu.VMEM((SAMPS, PANELS) + tile, F32),
            pltpu.VMEM((SAMPS, PANELS) + tile, F32),
            dma((PANELS,)), dma((PANELS,)), dma((2,)),
            dma((2, PANELS)), dma((2, PANELS)),
            dma((2,)), dma((TILES,)), dma((4,)), dma((4,)),
            dma((TILES,)), dma((2,)),
            dma((2,)), dma((2,)), dma((1,)), dma((1,)),
            dma((2,)), dma((TILES,)), dma((TILES,)), dma((2,)),
            dma((SAMPS,)), dma((SAMPS,)), dma((SAMPS,)), dma((SAMPS,)),
        ],
        compiler_params=pltpu.CompilerParams(
            collective_id=0, has_side_effects=True, vmem_limit_bytes=48 * 1024 * 1024
        ),
        cost_estimate=pl.CostEstimate(flops=200_000_000, bytes_accessed=7_000_000, transcendentals=0),
    )(bathymetry, initial_state, patterns, pattern_index, coupling, final_weights)


def solution(mesh):
    in_specs = (
        P(None, "tile", None),
        P(None, None, "tile", None),
        P(None, None, "tile", None),
        P("samp", None),
        P(),
        P("samp", None, None, "tile", None),
    )
    out_specs = P(None, "tile", None)
    return jax.shard_map(body, mesh=mesh, in_specs=in_specs, out_specs=out_specs, check_vma=False)
```

```python
import jax
import jax.numpy as jnp
from jax import lax
from jax.experimental import pallas as pl
from jax.experimental.pallas import tpu as pltpu
from jax.sharding import PartitionSpec as P

F32, BF16 = jnp.float32, jnp.bfloat16
MESH = pl.DeviceIdType.MESH
TILES, SAMPS, ROWS, CELLS, LAYERS, PANELS = 32, 8, 16, 512, 16, 6
LAST = TILES - 1


def split(x):
    high = x.astype(BF16)
    return high, (x - high.astype(F32)).astype(BF16)


def iota(shape, axis):
    return lax.broadcasted_iota(jnp.int32, shape, axis)


def dot(a, b):
    return jnp.dot(a, b, preferred_element_type=F32)


def kernel(
    depth_hbm, state_hbm, pattern_hbm, index_ref, coupling_ref, weight_hbm, out_ref,
    xs, ws, ps, bs, kz, kv, kq, field, qf, acc, acc_s, acc_n, ocs, leaving, pk, colh, gath, scat, prow, precv,
    mirror_out, mirror_in, hub_out, gath_p, scat_p, hub_in, part, rs_in, ag, done,
    load_x, load_w, load_pb, row_send, row_recv, hub_send, gath_recv, mir_send, mir_recv,
    scat_send, scat_recv, p_send, p_recv, pm_send, pm_recv, ph_send, pgath_recv, ps_send, ps_recv,
    rs_send, rs_recv, ag_send, ag_recv,
):
    t = lax.axis_index("tile")
    s = lax.axis_index("samp")
    left, right, mirror = (t + LAST) % TILES, (t + 1) % TILES, LAST - t
    is_first, is_last = t == 0, t == LAST
    is_hub = jnp.logical_or(is_first, is_last)
    at_end = t // LAST
    at_start = mirror // LAST

    def load(p):
        return (
            pltpu.make_async_copy(state_hbm.at[:, p], xs.at[p], load_x.at[p]),
            pltpu.make_async_copy(weight_hbm.at[0, :, p], ws.at[p], load_w.at[p]),
        )

    load_p = pltpu.make_async_copy(pattern_hbm, ps, load_pb.at[0])
    load_b = pltpu.make_async_copy(depth_hbm, bs, load_pb.at[1])
    for step in range(PANELS):
        for copy in load(PANELS - 1 - step):
            copy.start()
        if step == 0:
            load_p.start()
            load_b.start()

    barrier = pltpu.get_barrier_semaphore()

    def greet(device):
        pl.semaphore_signal(barrier, inc=1, device_id=device, device_id_type=MESH)

    def tell_tile(u, c):
        @pl.when(u != t)
        def _():
            greet({"tile": u})
        return c

    lax.fori_loop(0, TILES, tell_tile, 0)

    def tell_samp(u, c):
        @pl.when(u != s)
        def _():
            greet({"samp": u})
        return c

    lax.fori_loop(0, SAMPS, tell_samp, 0)

    mixing = coupling_ref[...] + jnp.where(iota((16, 16), 0) == iota((16, 16), 1), 1.0, 0.0)
    to_layer = (iota((256, 16), 0) % 16 == iota((256, 16), 1)).astype(BF16)
    from_layer = (iota((16, 256), 0) == iota((16, 256), 1) // 16).astype(BF16)
    same_row = iota((256, 256), 0) // 16 == iota((256, 256), 1) % 16

    def spread(matrix):
        tall = dot(to_layer, matrix).astype(BF16)
        return jnp.where(same_row, dot(tall, from_layer), 0.0).astype(BF16)

    for target, matrix in ((kz, mixing), (kv, mixing.T)):
        high, low = split(matrix)
        spread_high = spread(high)
        target[:, 0:256] = spread_high
        target[:, 256:512] = spread(low)
        target[:, 512:768] = spread_high
    thirty = jnp.where(
        jnp.logical_and(same_row, iota((256, 256), 0) % 16 == iota((256, 256), 1) // 16), 30.0, 0.0
    ).astype(BF16)
    kq[:, 0:256] = thirty
    kq[:, 256:512] = thirty
    chosen = (iota((4, 16), 0) == jnp.broadcast_to(index_ref[...], (4, 16))).astype(F32)
    tall = lax.dot_general(
        to_layer, chosen.astype(BF16), (((1,), (1,)), ((), ())), preferred_element_type=F32
    ).astype(BF16)
    from_pattern = (iota((4, 64), 0) == iota((4, 64), 1) // 16).astype(BF16)
    kq[:, 512:576] = jnp.where(
        iota((256, 64), 0) // 16 == iota((256, 64), 1) % 16, dot(tall, from_pattern), 0.0
    ).astype(BF16)

    acc_s[:, 1] = jnp.zeros((PANELS, 8, CELLS), F32)
    acc_n[:, 16] = jnp.zeros((PANELS, 8, CELLS), F32)
    lanes = iota((8, 128), 1)

    def remote(src, dst, send, recv, device):
        return pltpu.make_async_remote_copy(
            src_ref=src, dst_ref=dst, send_sem=send, recv_sem=recv,
            device_id=device, device_id_type=MESH,
        )

    def row_south(p):
        to = p + jnp.where(p < 4, at_end * ((p + 1) % 4 - p), 0)
        return remote(field.at[p, 16], field.at[to, 0], row_send.at[0, p], row_recv.at[0, to], {"tile": right})

    def row_north(p):
        to = p + jnp.where(p < 4, at_start * ((p + 3) % 4 - p), 0)
        return remote(field.at[p, 1], field.at[to, 17], row_send.at[1, p], row_recv.at[1, to], {"tile": left})

    def came_from_left(p):
        return remote(field.at[p, 16], field.at[p, 0], row_send.at[0, p], row_recv.at[0, p], {"tile": right})

    def came_from_right(p):
        return remote(field.at[p, 1], field.at[p, 17], row_send.at[1, p], row_recv.at[1, p], {"tile": left})

    def south_goes(p):
        return jnp.logical_or(p < 4, jnp.logical_not(is_last))

    def north_goes(p):
        return jnp.logical_or(p < 4, jnp.logical_not(is_first))

    def gather_to(hub):
        panel = 1 if hub else 3
        return remote(pk.at[panel], gath.at[t], hub_send.at[panel // 2], gath_recv.at[t], {"tile": hub})

    MIRRORED = (((2, 0), (5, 0)), ((2, 1), (4, 1)), ((5, 0), (2, 0)), ((4, 1), (2, 1)))

    def mirrored(n):
        (a, b), (c, d) = MIRRORED[n]
        return remote(pk.at[a, b], colh.at[c, d], mir_send.at[n], mir_recv.at[n], {"tile": mirror})

    def scatter_to(u, panel):
        return remote(scat.at[u], colh.at[panel], scat_send.at[u], scat_recv.at[panel // 2], {"tile": u})

    def seg_w(u):
        return jnp.where(is_last, LAST - u, u)

    def seg_e(u):
        return jnp.where(is_last, u, LAST - u)

    def make_scatter():
        slot = jnp.where(is_last, 16, 1)

        def one(u, c):
            for side in range(2):
                seg = seg_e(u) if side else seg_w(u)
                block, place = seg // 8, seg % 8
                out = jnp.zeros((8, 128), F32)
                for g in range(5):
                    x = field[5 - side, slot, pl.ds(8 * g, 8), pl.ds(pl.multiple_of(block * 128, 128), 128)]
                    x = pltpu.roll(x, (16 * g - 16 * place + 128) % 128, 1)
                    out = jnp.where(lanes // 16 == g, x, out)
                scat[u, side] = out

            @pl.when(jnp.logical_and(u != t, is_last))
            def _():
                scatter_to(u, 1).start()

            @pl.when(jnp.logical_and(u != t, is_first))
            def _():
                scatter_to(u, 3).start()

            return c

        lax.fori_loop(0, TILES, one, 0)

        @pl.when(is_last)
        def _():
            colh[1] = scat[t]

        @pl.when(is_first)
        def _():
            colh[3] = scat[t]

    def mix(step, c):
        p = PANELS - 1 - step
        for copy in load(p):
            copy.wait()
        xh, xl = split(xs[p].reshape(256, CELLS))
        z = dot(kz[...], jnp.concatenate([xh, xh, xl], 0))
        field[p, 1:17, 0:16, :] = z.reshape(ROWS, 16, CELLS)
        pat = ps[:, p].reshape(64, CELLS)
        q = dot(kq[...], jnp.concatenate([xh, xl, pat], 0))
        qf[p] = q.reshape(ROWS, 16, CELLS)
        wh, wl = split(ws[p].reshape(256, CELLS))
        v = dot(kv[...], jnp.concatenate([wh, wh, wl], 0))
        field[p, 1:17, 16:32, :] = v.reshape(ROWS, 16, CELLS)
        for i in range(ROWS):
            field[p, 1 + i, 32:40, :] = jnp.broadcast_to(0.5 * bs[p, i : i + 1, :], (8, CELLS))

        @pl.when(step == 0)
        def _():
            pl.semaphore_wait(barrier, TILES - 1 + SAMPS - 1)

        @pl.when(south_goes(p))
        def _():
            row_south(p).start()

        @pl.when(north_goes(p))
        def _():
            row_north(p).start()

        for side in range(2):
            if side == 0:
                rev = jnp.where(jnp.logical_or(p == 1, jnp.logical_or(p == 2, p == 5)), 1, 0)
            else:
                rev = jnp.where(jnp.logical_and(p >= 2, p <= 4), 1, 0)
            out = jnp.zeros((8, 128), F32)
            for i in range(ROWS):
                for g in range(5):
                    if side == 0:
                        x = field[p, 1 + i, 8 * g : 8 * g + 8, 0:128][:, 0:1]
                    else:
                        x = field[p, 1 + i, 8 * g : 8 * g + 8, CELLS - 128 : CELLS][:, 127:128]
                    spot = 16 * g + i + rev * (15 - 2 * i)
                    out = jnp.where(lanes == spot, jnp.broadcast_to(x, (8, 128)), out)
            pk[p, side] = out

        for at, hub in ((4, LAST), (2, 0)):
            @pl.when(jnp.logical_and(step == at, t != hub))
            def _():
                gather_to(hub).start()

            @pl.when(jnp.logical_and(step == at, t == hub))
            def _():
                gath[t] = pk[1 if hub else 3]

        @pl.when(jnp.logical_and(step == 1, is_hub))
        def _():
            make_scatter()

        @pl.when(step == 5)
        def _():
            for n in range(4):
                mirrored(n).start()

        return c

    load_p.wait()
    load_b.wait()
    lax.fori_loop(0, PANELS, mix, 0)

    colh[0, 0] = pk[5, 1]
    colh[0, 1] = pk[4, 0]
    colh[4, 0] = pk[0, 1]
    colh[5, 1] = pk[0, 0]

    first_lane, last_lane = lanes == 0, lanes == 127

    def block(g, p, slot, k):
        return field[p, slot, 8 * g : 8 * g + 8, 128 * k : 128 * k + 128]

    def stencil_row(p, i):
        slot = i + 1
        west, east = colh[p, 0], colh[p, 1]
        at = {}

        def here(g, k):
            if (g, k) not in at:
                x = block(g, p, slot, k)
                at[g, k] = x, pltpu.roll(x, 127, 1)
            return at[g, k]

        def east_of(g, k):
            x, turned = here(g, k)
            if k < 3:
                after = here(g, k + 1)[1]
            else:
                after = pltpu.roll(east, (127 - 16 * g - i) % 128, 1)
            return x, jnp.where(last_lane, after, turned)

        before = {}

        def west_of(g, k, value, x):
            turned = pltpu.roll(value, 1, 1)
            if k == 0:
                edge = pltpu.roll(west, (128 - 16 * g - i) % 128, 1)
                edge = x + edge if g == 4 else x - edge
            else:
                edge = before[g]
            before[g] = turned
            return jnp.where(first_lane, edge, turned)

        held = {}
        for k in range(4):
            x, e = east_of(4, k)
            beta_e = x + e
            beta_w = west_of(4, k, beta_e, x)
            beta_s = x + block(4, p, slot + 1, k)
            beta_n = x + block(4, p, slot - 1, k)
            sums = None
            for half in range(2):
                both = []
                for g in (half, 2 + half):
                    x, e = east_of(g, k)
                    de = e - x
                    dw = west_of(g, k, de, x)
                    ds = block(g, p, slot + 1, k) - x
                    dn = x - block(g, p, slot - 1, k)
                    lap = (beta_e * de - beta_w * dw) + (beta_s * ds - beta_n * dn)
                    both.append((lap, de, dw, ds, dn))
                (lz, *dz), (lv, *dv) = both
                q = lz + qf[p, i, 8 * half : 8 * half + 8, 128 * k : 128 * k + 128]
                terms = [x * q + y * lv for x, y in zip(dv, dz)]
                sums = terms if sums is None else [x + y for x, y in zip(sums, terms)]
            pe, pw, p_s, p_n = sums
            cols = slice(128 * k, 128 * k + 128)
            acc_s[p, slot + 1, :, cols] = p_s
            acc_n[p, slot - 1, :, cols] = p_n
            own = (pe + p_s) - (pw + p_n)
            pe_turned = pltpu.roll(pe, 1, 1)
            own = own + jnp.where(first_lane, held["e"] if k else 0.0, pe_turned)
            pw_turned = pltpu.roll(pw, 127, 1)
            if k == 0:
                first = pw_turned
            else:
                acc[p, slot, :, 128 * k - 128 : 128 * k] = held["own"] - jnp.where(
                    last_lane, pw_turned, held["w"]
                )
            held = {"e": pe_turned, "w": pw_turned, "own": own}
        acc[p, slot, :, 384:512] = held["own"] - jnp.where(last_lane, 0.0, held["w"])
        ocs[p, i] = jnp.where(first_lane, held["e"], jnp.where(last_lane, -first, 0.0))

    def stencil_rows(p, start, count):
        for r in range(count):
            stencil_row(p, start + r)

    def wait_columns():
        for n in range(4):
            mirrored(n).wait_recv()

        @pl.when(t != LAST)
        def _():
            scatter_to(LAST, 1).wait_recv()

        @pl.when(t != 0)
        def _():
            scatter_to(0, 3).wait_recv()

        turn(1, 0)
        turn(3, 1)

    def turn(p, side):
        x = colh[p, side]
        out = x
        for e in range(16):
            out = jnp.where(lanes % 16 == 15 - e, pltpu.roll(x, (15 - 2 * e) % 128, 1), out)
        colh[p, side] = out

    def inner(p, c):
        @pl.when(p == 1)
        def _():
            wait_columns()

        def two(n, c):
            stencil_rows(p, 1 + 2 * n, 2)
            return c

        lax.fori_loop(0, 7, two, 0)
        return c

    lax.fori_loop(0, 4, inner, 0)

    @pl.when(is_hub)
    def _():
        def wait_one(u, c):
            @pl.when(u != t)
            def _():
                remote(pk.at[1], gath.at[u], hub_send.at[0], gath_recv.at[u], {"tile": u}).wait_recv()
            return c

        lax.fori_loop(0, TILES, wait_one, 0)
        slot = jnp.where(is_last, 17, 0)

        def one(block, c):
            for side in range(2):
                for g in range(5):
                    out = jnp.zeros((8, 128), F32)
                    for k in range(8):
                        seg = 8 * block + k
                        u = seg_e(seg) if side else seg_w(seg)
                        x = pltpu.roll(gath[u, side], (16 * k - 16 * g + 128) % 128, 1)
                        out = jnp.where(lanes // 16 == k, x, out)
                    field[5 - side, slot, pl.ds(8 * g, 8), pl.ds(pl.multiple_of(block * 128, 128), 128)] = out
            return c

        lax.fori_loop(0, 4, one, 0)

    def outer(p, c):
        @pl.when(jnp.logical_or(p < 4, jnp.logical_not(is_first)))
        def _():
            came_from_left(p).wait_recv()

        @pl.when(jnp.logical_or(p < 4, jnp.logical_not(is_last)))
        def _():
            came_from_right(p).wait_recv()

        stencil_rows(p, 0, 1)
        stencil_rows(p, ROWS - 1, 1)
        return c

    lax.fori_loop(0, PANELS, outer, 0)

    def fold(matrix, x):
        high, low = split(x)
        return dot(matrix, high) + dot(matrix, low)

    fold_rows = (iota((ROWS, 8 * ROWS), 0) == iota((ROWS, 8 * ROWS), 1) // 8).astype(BF16)
    fold_panels = (iota((8, 8 * PANELS), 0) == iota((8, 8 * PANELS), 1) // 8).astype(BF16)
    lane16, row16 = iota((16, 128), 1), iota((16, 128), 0)

    prow[0] = -fold(fold_panels, acc_n[:, 0].reshape(8 * PANELS, CELLS))
    prow[1] = fold(fold_panels, acc_s[:, 17].reshape(8 * PANELS, CELLS))
    p_south = remote(prow.at[1], precv.at[0], p_send.at[0], p_recv.at[0], {"tile": right})
    p_north = remote(prow.at[0], precv.at[1], p_send.at[1], p_recv.at[1], {"tile": left})
    p_south.start()
    p_north.start()

    def fold_leaving(p, c):
        leaving[p] = fold(fold_rows, ocs[p].reshape(8 * ROWS, 128))
        return c

    lax.fori_loop(1, 4, fold_leaving, 0)

    def leaving_column(p, side):
        return leaving[p][:, 0:1] if side else leaving[p][:, 127:128]

    def leaving_row(p, side, reverse):
        spot = 15 - row16 if reverse else row16
        column = jnp.broadcast_to(leaving_column(p, side), (16, 128))
        return jnp.sum(jnp.where(lane16 == spot, column, 0.0), axis=0, keepdims=True)

    def p_mirror(m):
        return remote(mirror_out.at[m], mirror_in.at[m], pm_send.at[m], pm_recv.at[m], {"tile": mirror})

    def send_mirror(m):
        mirror_out[m] = jnp.zeros((8, 128), F32)
        for n in range(2):
            (a, b), _ = MIRRORED[2 * m + n]
            mirror_out[m, n : n + 1, :] = leaving_row(a, b, True)
        p_mirror(m).start()

    send_mirror(0)

    def gather_p(hub):
        n = 0 if hub else 1
        return remote(hub_out.at[n], gath_p.at[t], ph_send.at[n], pgath_recv.at[t], {"tile": hub})

    up, down = t % 8, (LAST - t) % 8
    for n, hub in enumerate((LAST, 0)):
        panel = 1 if hub else 3
        hub_out[n] = jnp.zeros((8, 128), F32)
        hub_out[n, 0:1, :] = pltpu.roll(leaving_row(panel, 0, bool(hub)), 16 * (down if hub else up), 1)
        hub_out[n, 1:2, :] = pltpu.roll(leaving_row(panel, 1, not hub), 16 * (up if hub else down), 1)

        @pl.when(t != hub)
        def _():
            gather_p(hub).start()

        @pl.when(t == hub)
        def _():
            gath_p[t] = hub_out[n]

    def scatter_p(u, hub):
        n = 0 if hub else 1
        return remote(scat_p.at[u // 8], hub_in.at[n], ps_send.at[u], ps_recv.at[n], {"tile": u})

    @pl.when(is_hub)
    def _():
        rows = prow[jnp.where(is_last, 1, 0)]
        for block_at in range(4):
            ahead = rows[:, 128 * block_at : 128 * block_at + 128]
            behind = rows[:, 128 * (3 - block_at) : 128 * (3 - block_at) + 128]
            w = jnp.where(is_last, behind, ahead)
            e = jnp.where(is_last, ahead, behind)
            scat_p[block_at] = jnp.zeros((8, 128), F32)
            scat_p[block_at, 0:1, :] = w[5:6]
            scat_p[block_at, 1:2, :] = e[4:5]

        def one(u, c):
            @pl.when(jnp.logical_and(u != t, is_last))
            def _():
                scatter_p(u, LAST).start()

            @pl.when(jnp.logical_and(u != t, is_first))
            def _():
                scatter_p(u, 0).start()

            return c

        lax.fori_loop(0, TILES, one, 0)

        @pl.when(is_last)
        def _():
            hub_in[0] = scat_p[t // 8]

        @pl.when(is_first)
        def _():
            hub_in[1] = scat_p[t // 8]

    lax.fori_loop(4, PANELS, inner, 0)
    lax.fori_loop(3, PANELS, lambda n, c: fold_leaving(n * (n // 4), c), 0)
    send_mirror(1)

    def fold_part(p, c):
        mine = acc[p, 1:17] + (acc_s[p, 1:17] - acc_n[p, 1:17])
        part[p] = fold(fold_rows, mine.reshape(8 * ROWS, CELLS))
        return c

    lax.fori_loop(0, PANELS, fold_part, 0)

    def add_column(p, side, column):
        if side:
            at, lane = CELLS - 128, 127
        else:
            at, lane = 0, 0
        spread_out = jnp.broadcast_to(column, (16, 128))
        part[p, :, at : at + 128] += jnp.where(lane16 == lane, spread_out, 0.0)

    add_column(5, 1, leaving_column(0, 0))
    add_column(4, 0, leaving_column(0, 1))
    add_column(0, 1, leaving_column(4, 0))
    add_column(0, 0, leaving_column(5, 1))

    def row_to_column(row, base, reverse):
        spot = base + (15 - row16 if reverse else row16)
        spread_out = jnp.broadcast_to(row, (16, 128))
        return jnp.sum(jnp.where(lane16 == spot, spread_out, 0.0), axis=1, keepdims=True)

    p_south.wait_recv()
    p_north.wait_recv()
    from_north = precv[0]
    from_south = precv[1]
    pad = jnp.zeros((4, CELLS), F32)
    from_north = jnp.where(is_first, jnp.concatenate([from_north[3:4], from_north[0:3], pad], 0), from_north)
    from_south = jnp.where(is_last, jnp.concatenate([from_south[1:4], from_south[0:1], pad], 0), from_south)
    for p in range(PANELS):
        part[p, 0:1, :] += from_north[p : p + 1]
        part[p, ROWS - 1 : ROWS, :] += from_south[p : p + 1]

    def from_mirror(m):
        p_mirror(m).wait_recv()
        for n in range(2):
            _, (a, b) = MIRRORED[2 * m + n]
            add_column(a, b, row_to_column(mirror_in[m, n : n + 1, :], 0, False))

    from_mirror(0)

    @pl.when(is_hub)
    def _():
        def wait_one(u, c):
            @pl.when(u != t)
            def _():
                remote(hub_out.at[0], gath_p.at[u], ph_send.at[0], pgath_recv.at[u], {"tile": u}).wait_recv()
            return c

        lax.fori_loop(0, TILES, wait_one, 0)
        row_at = jnp.where(is_last, ROWS - 1, 0)
        for block_at in range(4):
            cols = slice(128 * block_at, 128 * block_at + 128)
            for side in range(2):
                total = jnp.zeros((8, 128), F32)
                for k in range(8):
                    seg = 8 * block_at + k
                    total = total + gath_p[seg_e(seg) if side else seg_w(seg)]
                row = jnp.broadcast_to(total[side : side + 1, :], (16, 128))
                part[5 - side, :, cols] += jnp.where(row16 == row_at, row, 0.0)

    GROUPS = ((0, 4, 5), (1, 2, 3))

    def each_peer(fn):
        def one(d, c):
            fn((s + d) % SAMPS)
            return c

        lax.fori_loop(1, SAMPS, one, 0)

    def reduce_to(m, peer):
        return remote(rs_in.at[m, peer], ag.at[m, s], rs_send.at[m, peer], rs_recv.at[m, s], {"samp": peer})

    def reduce_from(m, peer):
        return remote(rs_in.at[m, peer], ag.at[m, peer], rs_send.at[m, peer], rs_recv.at[m, peer], {"samp": peer})

    def share_with(m, peer):
        return remote(done.at[m, s], done.at[m, s], ag_send.at[m, peer], ag_recv.at[m, s], {"samp": peer})

    def share_from(m, peer):
        return remote(done.at[m, peer], done.at[m, peer], ag_send.at[m, peer], ag_recv.at[m, peer], {"samp": peer})

    def reduce_start(m):
        for n in range(SAMPS):
            h, k = n // 4, n % 4
            for j, p in enumerate(GROUPS[m]):
                rs_in[m, n, j] = part[p, 8 * h : 8 * h + 8, 128 * k : 128 * k + 128]
        each_peer(lambda peer: reduce_to(m, peer).start())
        ag[m, s] = rs_in[m, s]

    def reduce_end(m):
        each_peer(lambda peer: reduce_from(m, peer).wait_recv())
        total = ag[m, 0]
        for n in range(1, SAMPS):
            total = total + ag[m, n]
        done[m, s] = total * (0.005 / SAMPS)
        each_peer(lambda peer: share_with(m, peer).start())

    reduce_start(0)

    @pl.when(t != LAST)
    def _():
        scatter_p(LAST, LAST).wait_recv()

    @pl.when(t != 0)
    def _():
        scatter_p(0, 0).wait_recv()

    add_column(1, 0, row_to_column(hub_in[0, 0:1, :], 16 * down, True))
    add_column(1, 1, row_to_column(hub_in[0, 1:2, :], 16 * up, False))
    add_column(3, 0, row_to_column(hub_in[1, 0:1, :], 16 * up, False))
    add_column(3, 1, row_to_column(hub_in[1, 1:2, :], 16 * down, True))
    from_mirror(1)
    reduce_start(1)
    reduce_end(0)
    reduce_end(1)
    for m in range(2):
        each_peer(lambda peer: share_from(m, peer).wait_recv())
        for n in range(SAMPS):
            h, k = n // 4, n % 4
            for j, p in enumerate(GROUPS[m]):
                out_ref[p, 8 * h : 8 * h + 8, 128 * k : 128 * k + 128] = done[m, n, j]

    for m in range(2):
        each_peer(lambda peer: reduce_to(m, peer).wait_send())
        each_peer(lambda peer: share_with(m, peer).wait_send())
        p_mirror(m).wait_send()

    def rows_left(p, c):
        @pl.when(south_goes(p))
        def _():
            row_south(p).wait_send()

        @pl.when(north_goes(p))
        def _():
            row_north(p).wait_send()

        return c

    lax.fori_loop(0, PANELS, rows_left, 0)
    for n in range(4):
        mirrored(n).wait_send()
    p_south.wait_send()
    p_north.wait_send()
    for hub in (LAST, 0):
        @pl.when(t != hub)
        def _():
            gather_to(hub).wait_send()
            gather_p(hub).wait_send()

    @pl.when(is_hub)
    def _():
        def one(u, c):
            @pl.when(u != t)
            def _():
                scatter_to(u, 1).wait_send()
                scatter_p(u, LAST).wait_send()
            return c

        lax.fori_loop(0, TILES, one, 0)


def body(bathymetry, initial_state, patterns, pattern_index, coupling, final_weights):
    vmem = pl.BlockSpec(memory_space=pltpu.VMEM)
    hbm = pl.BlockSpec(memory_space=pl.ANY)
    tile = (8, 128)
    dma = pltpu.SemaphoreType.DMA
    return pl.pallas_call(
        kernel,
        out_shape=jax.ShapeDtypeStruct((PANELS, ROWS, CELLS), F32),
        in_specs=[hbm, hbm, hbm, vmem, vmem, hbm],
        out_specs=vmem,
        scratch_shapes=[
            pltpu.VMEM((PANELS, LAYERS, ROWS, CELLS), F32),
            pltpu.VMEM((PANELS, LAYERS, ROWS, CELLS), F32),
            pltpu.VMEM((4, PANELS, ROWS, CELLS), BF16),
            pltpu.VMEM((PANELS, ROWS, CELLS), F32),
            pltpu.VMEM((256, 768), BF16),
            pltpu.VMEM((256, 768), BF16),
            pltpu.VMEM((256, 576), BF16),
            pltpu.VMEM((PANELS, ROWS + 2, 40, CELLS), F32),
            pltpu.VMEM((PANELS, ROWS, LAYERS, CELLS), F32),
            pltpu.VMEM((PANELS, ROWS + 2, 8, CELLS), F32),
            pltpu.VMEM((PANELS, ROWS + 2, 8, CELLS), F32),
            pltpu.VMEM((PANELS, ROWS + 2, 8, CELLS), F32),
            pltpu.VMEM((PANELS, ROWS) + tile, F32),
            pltpu.VMEM((PANELS, ROWS, 128), F32),
            pltpu.VMEM((PANELS, 2) + tile, F32),
            pltpu.VMEM((PANELS, 2) + tile, F32),
            pltpu.VMEM((TILES, 2) + tile, F32),
            pltpu.VMEM((TILES, 2) + tile, F32),
            pltpu.VMEM((2, 8, CELLS), F32),
            pltpu.VMEM((2, 8, CELLS), F32),
            pltpu.VMEM((2,) + tile, F32),
            pltpu.VMEM((2,) + tile, F32),
            pltpu.VMEM((2,) + tile, F32),
            pltpu.VMEM((TILES,) + tile, F32),
            pltpu.VMEM((4,) + tile, F32),
            pltpu.VMEM((2,) + tile, F32),
            pltpu.VMEM((PANELS, ROWS, CELLS), F32),
            pltpu.VMEM((2, SAMPS, 3) + tile, F32),
            pltpu.VMEM((2, SAMPS, 3) + tile, F32),
            pltpu.VMEM((2, SAMPS, 3) + tile, F32),
            dma((PANELS,)), dma((PANELS,)), dma((2,)),
            dma((2, PANELS)), dma((2, PANELS)),
            dma((2,)), dma((TILES,)), dma((4,)), dma((4,)),
            dma((TILES,)), dma((2,)),
            dma((2,)), dma((2,)), dma((2,)), dma((2,)),
            dma((2,)), dma((TILES,)), dma((TILES,)), dma((2,)),
            dma((2, SAMPS)), dma((2, SAMPS)), dma((2, SAMPS)), dma((2, SAMPS)),
        ],
        compiler_params=pltpu.CompilerParams(
            collective_id=0, has_side_effects=True, vmem_limit_bytes=56 * 1024 * 1024
        ),
        cost_estimate=pl.CostEstimate(flops=200_000_000, bytes_accessed=7_000_000, transcendentals=0),
    )(bathymetry, initial_state, patterns, pattern_index, coupling, final_weights)


def solution(mesh):
    in_specs = (
        P(None, "tile", None),
        P(None, None, "tile", None),
        P(None, None, "tile", None),
        P("samp", None),
        P(),
        P("samp", None, None, "tile", None),
    )
    out_specs = P(None, "tile", None)
    return jax.shard_map(body, mesh=mesh, in_specs=in_specs, out_specs=out_specs, check_vma=False)
```

```python
import jax
import jax.numpy as jnp
from jax import lax
from jax.experimental import pallas as pl
from jax.experimental.pallas import tpu as pltpu
from jax.sharding import PartitionSpec as P

F32, BF16 = jnp.float32, jnp.bfloat16
MESH = pl.DeviceIdType.MESH
TILES, SAMPS, ROWS, CELLS, LAYERS, PANELS = 32, 8, 16, 512, 16, 6
LAST = TILES - 1


def split(x):
    high = x.astype(BF16)
    return high, (x - high.astype(F32)).astype(BF16)


def iota(shape, axis):
    return lax.broadcasted_iota(jnp.int32, shape, axis)


def dot(a, b):
    return jnp.dot(a, b, preferred_element_type=F32)


def kernel(
    depth_hbm, state_hbm, pattern_hbm, index_ref, coupling_ref, weight_hbm, out_ref,
    xs, ws, ps, bs, kz, kv, kq, field, qf, acc_e, acc_w, acc_s, acc_n, sum_e, sum_w, pk, colh, gath, scat, prow, precv,
    mirror_out, mirror_in, hub_out, gath_p, scat_p, hub_in, part, rs_in, ag, done,
    load_x, load_w, load_pb, row_send, row_recv, hub_send, gath_recv, mir_send, mir_recv,
    scat_send, scat_recv, p_send, p_recv, pm_send, pm_recv, ph_send, pgath_recv, ps_send, ps_recv,
    rs_send, rs_recv, ag_send, ag_recv,
):
    t = lax.axis_index("tile")
    s = lax.axis_index("samp")
    left, right, mirror = (t + LAST) % TILES, (t + 1) % TILES, LAST - t
    is_first, is_last = t == 0, t == LAST
    is_hub = jnp.logical_or(is_first, is_last)
    at_end = t // LAST
    at_start = mirror // LAST

    def load(p):
        return (
            pltpu.make_async_copy(state_hbm.at[:, p], xs.at[p], load_x.at[p]),
            pltpu.make_async_copy(weight_hbm.at[0, :, p], ws.at[p], load_w.at[p]),
        )

    load_p = pltpu.make_async_copy(pattern_hbm, ps, load_pb.at[0])
    load_b = pltpu.make_async_copy(depth_hbm, bs, load_pb.at[1])
    for step in range(PANELS):
        for copy in load(PANELS - 1 - step):
            copy.start()
        if step == 0:
            load_p.start()
            load_b.start()

    barrier = pltpu.get_barrier_semaphore()

    def greet(device):
        pl.semaphore_signal(barrier, inc=1, device_id=device, device_id_type=MESH)

    def tell_tile(u, c):
        @pl.when(u != t)
        def _():
            greet({"tile": u})
        return c

    lax.fori_loop(0, TILES, tell_tile, 0)

    def tell_samp(u, c):
        @pl.when(u != s)
        def _():
            greet({"samp": u})
        return c

    lax.fori_loop(0, SAMPS, tell_samp, 0)

    mixing = coupling_ref[...] + jnp.where(iota((16, 16), 0) == iota((16, 16), 1), 1.0, 0.0)
    to_layer = (iota((256, 16), 0) % 16 == iota((256, 16), 1)).astype(BF16)
    from_layer = (iota((16, 256), 0) == iota((16, 256), 1) // 16).astype(BF16)
    same_row = iota((256, 256), 0) // 16 == iota((256, 256), 1) % 16

    def spread(matrix):
        tall = dot(to_layer, matrix).astype(BF16)
        return jnp.where(same_row, dot(tall, from_layer), 0.0).astype(BF16)

    for target, matrix in ((kz, mixing), (kv, mixing.T)):
        high, low = split(matrix)
        spread_high = spread(high)
        target[:, 0:256] = spread_high
        target[:, 256:512] = spread(low)
        target[:, 512:768] = spread_high
    thirty = jnp.where(
        jnp.logical_and(same_row, iota((256, 256), 0) % 16 == iota((256, 256), 1) // 16), 30.0, 0.0
    ).astype(BF16)
    kq[:, 0:256] = thirty
    kq[:, 256:512] = thirty
    chosen = (iota((4, 16), 0) == jnp.broadcast_to(index_ref[...], (4, 16))).astype(F32)
    tall = lax.dot_general(
        to_layer, chosen.astype(BF16), (((1,), (1,)), ((), ())), preferred_element_type=F32
    ).astype(BF16)
    from_pattern = (iota((4, 64), 0) == iota((4, 64), 1) // 16).astype(BF16)
    kq[:, 512:576] = jnp.where(
        iota((256, 64), 0) // 16 == iota((256, 64), 1) % 16, dot(tall, from_pattern), 0.0
    ).astype(BF16)

    acc_s[:, 1] = jnp.zeros((PANELS, 8, CELLS), F32)
    acc_n[:, 16] = jnp.zeros((PANELS, 8, CELLS), F32)
    lanes = iota((8, 128), 1)

    def remote(src, dst, send, recv, device):
        return pltpu.make_async_remote_copy(
            src_ref=src, dst_ref=dst, send_sem=send, recv_sem=recv,
            device_id=device, device_id_type=MESH,
        )

    def row_south(p):
        to = p + jnp.where(p < 4, at_end * ((p + 1) % 4 - p), 0)
        return remote(field.at[p, 16], field.at[to, 0], row_send.at[0, p], row_recv.at[0, to], {"tile": right})

    def row_north(p):
        to = p + jnp.where(p < 4, at_start * ((p + 3) % 4 - p), 0)
        return remote(field.at[p, 1], field.at[to, 17], row_send.at[1, p], row_recv.at[1, to], {"tile": left})

    def came_from_left(p):
        return remote(field.at[p, 16], field.at[p, 0], row_send.at[0, p], row_recv.at[0, p], {"tile": right})

    def came_from_right(p):
        return remote(field.at[p, 1], field.at[p, 17], row_send.at[1, p], row_recv.at[1, p], {"tile": left})

    def south_goes(p):
        return jnp.logical_or(p < 4, jnp.logical_not(is_last))

    def north_goes(p):
        return jnp.logical_or(p < 4, jnp.logical_not(is_first))

    def gather_to(hub):
        panel = 1 if hub else 3
        return remote(pk.at[panel], gath.at[t], hub_send.at[panel // 2], gath_recv.at[t], {"tile": hub})

    MIRRORED = (((2, 0), (5, 0)), ((2, 1), (4, 1)), ((5, 0), (2, 0)), ((4, 1), (2, 1)))

    def mirrored(n):
        (a, b), (c, d) = MIRRORED[n]
        return remote(pk.at[a, b], colh.at[c, d], mir_send.at[n], mir_recv.at[n], {"tile": mirror})

    def scatter_to(u, panel):
        return remote(scat.at[u], colh.at[panel], scat_send.at[u], scat_recv.at[panel // 2], {"tile": u})

    def seg_w(u):
        return jnp.where(is_last, LAST - u, u)

    def seg_e(u):
        return jnp.where(is_last, u, LAST - u)

    def make_scatter():
        slot = jnp.where(is_last, 16, 1)

        def one(u, c):
            for side in range(2):
                seg = seg_e(u) if side else seg_w(u)
                block, place = seg // 8, seg % 8
                out = jnp.zeros((8, 128), F32)
                for g in range(5):
                    x = field[5 - side, slot, pl.ds(8 * g, 8), pl.ds(pl.multiple_of(block * 128, 128), 128)]
                    x = pltpu.roll(x, (16 * g - 16 * place + 128) % 128, 1)
                    out = jnp.where(lanes // 16 == g, x, out)
                scat[u, side] = out

            @pl.when(jnp.logical_and(u != t, is_last))
            def _():
                scatter_to(u, 1).start()

            @pl.when(jnp.logical_and(u != t, is_first))
            def _():
                scatter_to(u, 3).start()

            return c

        lax.fori_loop(0, TILES, one, 0)

        @pl.when(is_last)
        def _():
            colh[1] = scat[t]

        @pl.when(is_first)
        def _():
            colh[3] = scat[t]

    def mix(step, c):
        p = PANELS - 1 - step
        for copy in load(p):
            copy.wait()
        xh, xl = split(xs[p].reshape(256, CELLS))
        z = dot(kz[...], jnp.concatenate([xh, xh, xl], 0))
        field[p, 1:17, 0:16, :] = z.reshape(ROWS, 16, CELLS)
        pat = ps[:, p].reshape(64, CELLS)
        q = dot(kq[...], jnp.concatenate([xh, xl, pat], 0))
        qf[p] = q.reshape(ROWS, 16, CELLS)
        wh, wl = split(ws[p].reshape(256, CELLS))
        v = dot(kv[...], jnp.concatenate([wh, wh, wl], 0))
        field[p, 1:17, 16:32, :] = v.reshape(ROWS, 16, CELLS)
        for i in range(ROWS):
            field[p, 1 + i, 32:40, :] = jnp.broadcast_to(0.5 * bs[p, i : i + 1, :], (8, CELLS))

        @pl.when(step == 0)
        def _():
            pl.semaphore_wait(barrier, TILES - 1 + SAMPS - 1)

        @pl.when(south_goes(p))
        def _():
            row_south(p).start()

        @pl.when(north_goes(p))
        def _():
            row_north(p).start()

        for side in range(2):
            if side == 0:
                rev = jnp.where(jnp.logical_or(p == 1, jnp.logical_or(p == 2, p == 5)), 1, 0)
            else:
                rev = jnp.where(jnp.logical_and(p >= 2, p <= 4), 1, 0)
            out = jnp.zeros((8, 128), F32)
            for i in range(ROWS):
                for g in range(5):
                    if side == 0:
                        x = field[p, 1 + i, 8 * g : 8 * g + 8, 0:128][:, 0:1]
                    else:
                        x = field[p, 1 + i, 8 * g : 8 * g + 8, CELLS - 128 : CELLS][:, 127:128]
                    spot = 16 * g + i + rev * (15 - 2 * i)
                    out = jnp.where(lanes == spot, jnp.broadcast_to(x, (8, 128)), out)
            pk[p, side] = out

        for at, hub in ((4, LAST), (2, 0)):
            @pl.when(jnp.logical_and(step == at, t != hub))
            def _():
                gather_to(hub).start()

            @pl.when(jnp.logical_and(step == at, t == hub))
            def _():
                gath[t] = pk[1 if hub else 3]

        @pl.when(jnp.logical_and(step == 1, is_hub))
        def _():
            make_scatter()

        @pl.when(step == 5)
        def _():
            for n in range(4):
                mirrored(n).start()

        return c

    load_p.wait()
    load_b.wait()
    lax.fori_loop(0, PANELS, mix, 0)

    colh[0, 0] = pk[5, 1]
    colh[0, 1] = pk[4, 0]
    colh[4, 0] = pk[0, 1]
    colh[5, 1] = pk[0, 0]

    first_lane, last_lane = lanes == 0, lanes == 127

    def block(g, p, slot, k):
        return field[p, slot, 8 * g : 8 * g + 8, 128 * k : 128 * k + 128]

    def stencil_row(p, i):
        slot = i + 1
        west, east = colh[p, 0], colh[p, 1]

        def sides(g):
            x = [block(g, p, slot, k) for k in range(4)]
            r = [pltpu.roll(y, 127, 1) for y in x] + [pltpu.roll(east, (127 - 16 * g - i) % 128, 1)]
            l = [pltpu.roll(west, (128 - 16 * g - i) % 128, 1)] + [pltpu.roll(y, 1, 1) for y in x]
            return (
                x,
                [jnp.where(last_lane, r[k + 1], r[k]) for k in range(4)],
                [jnp.where(first_lane, l[k], l[k + 1]) for k in range(4)],
            )

        every = [sides(g) for g in range(5)]
        for k in range(4):
            x, e, w = (v[k] for v in every[4])
            beta_e = x + e
            beta_w = x + w
            beta_s = x + block(4, p, slot + 1, k)
            beta_n = x + block(4, p, slot - 1, k)
            sums = None
            for half in range(2):
                both = []
                for g in (half, 2 + half):
                    x, e, w = (v[k] for v in every[g])
                    de = e - x
                    dw = x - w
                    ds = block(g, p, slot + 1, k) - x
                    dn = x - block(g, p, slot - 1, k)
                    lap = (beta_e * de - beta_w * dw) + (beta_s * ds - beta_n * dn)
                    both.append((lap, de, dw, ds, dn))
                (lz, *dz), (lv, *dv) = both
                q = lz + qf[p, i, 8 * half : 8 * half + 8, 128 * k : 128 * k + 128]
                terms = [x * q + y * lv for x, y in zip(dv, dz)]
                sums = terms if sums is None else [x + y for x, y in zip(sums, terms)]
            cols = slice(128 * k, 128 * k + 128)
            acc_e[p, i, :, cols] = sums[0]
            acc_w[p, i, :, cols] = sums[1]
            acc_s[p, slot + 1, :, cols] = sums[2]
            acc_n[p, slot - 1, :, cols] = sums[3]

    def stencil_rows(p, start, count):
        for r in range(count):
            stencil_row(p, start + r)

    def wait_columns():
        for n in range(4):
            mirrored(n).wait_recv()

        @pl.when(t != LAST)
        def _():
            scatter_to(LAST, 1).wait_recv()

        @pl.when(t != 0)
        def _():
            scatter_to(0, 3).wait_recv()

        turn(1, 0)
        turn(3, 1)

    def turn(p, side):
        x = colh[p, side]
        out = x
        for e in range(16):
            out = jnp.where(lanes % 16 == 15 - e, pltpu.roll(x, (15 - 2 * e) % 128, 1), out)
        colh[p, side] = out

    def inner(p, c):
        @pl.when(p == 1)
        def _():
            wait_columns()

        def seven(n, c):
            stencil_rows(p, 1 + 7 * n, 7)
            return c

        lax.fori_loop(0, 2, seven, 0)
        return c

    lax.fori_loop(0, 4, inner, 0)

    @pl.when(is_hub)
    def _():
        def wait_one(u, c):
            @pl.when(u != t)
            def _():
                remote(pk.at[1], gath.at[u], hub_send.at[0], gath_recv.at[u], {"tile": u}).wait_recv()
            return c

        lax.fori_loop(0, TILES, wait_one, 0)
        slot = jnp.where(is_last, 17, 0)

        def one(block, c):
            for side in range(2):
                for g in range(5):
                    out = jnp.zeros((8, 128), F32)
                    for k in range(8):
                        seg = 8 * block + k
                        u = seg_e(seg) if side else seg_w(seg)
                        x = pltpu.roll(gath[u, side], (16 * k - 16 * g + 128) % 128, 1)
                        out = jnp.where(lanes // 16 == k, x, out)
                    field[5 - side, slot, pl.ds(8 * g, 8), pl.ds(pl.multiple_of(block * 128, 128), 128)] = out
            return c

        lax.fori_loop(0, 4, one, 0)

    def outer(p, c):
        @pl.when(jnp.logical_or(p < 4, jnp.logical_not(is_first)))
        def _():
            came_from_left(p).wait_recv()

        @pl.when(jnp.logical_or(p < 4, jnp.logical_not(is_last)))
        def _():
            came_from_right(p).wait_recv()

        stencil_rows(p, 0, 1)
        stencil_rows(p, ROWS - 1, 1)
        return c

    lax.fori_loop(0, PANELS, outer, 0)

    def fold(matrix, x):
        high, low = split(x)
        return dot(matrix, high) + dot(matrix, low)

    fold_rows = (iota((ROWS, 8 * ROWS), 0) == iota((ROWS, 8 * ROWS), 1) // 8).astype(BF16)
    fold_panels = (iota((8, 8 * PANELS), 0) == iota((8, 8 * PANELS), 1) // 8).astype(BF16)
    lane16, row16 = iota((16, 128), 1), iota((16, 128), 0)

    prow[0] = -fold(fold_panels, acc_n[:, 0].reshape(8 * PANELS, CELLS))
    prow[1] = fold(fold_panels, acc_s[:, 17].reshape(8 * PANELS, CELLS))
    p_south = remote(prow.at[1], precv.at[0], p_send.at[0], p_recv.at[0], {"tile": right})
    p_north = remote(prow.at[0], precv.at[1], p_send.at[1], p_recv.at[1], {"tile": left})
    p_south.start()
    p_north.start()

    def fold_leaving(p, c):
        sum_e[p] = fold(fold_rows, acc_e[p].reshape(8 * ROWS, CELLS))
        sum_w[p] = fold(fold_rows, acc_w[p].reshape(8 * ROWS, CELLS))
        return c

    lax.fori_loop(1, 4, fold_leaving, 0)

    def leaving_column(p, side):
        return sum_e[p, :, CELLS - 128 :][:, 127:128] if side else -sum_w[p, :, 0:128][:, 0:1]

    def leaving_row(p, side, reverse):
        spot = 15 - row16 if reverse else row16
        column = jnp.broadcast_to(leaving_column(p, side), (16, 128))
        return jnp.sum(jnp.where(lane16 == spot, column, 0.0), axis=0, keepdims=True)

    def p_mirror(m):
        return remote(mirror_out.at[m], mirror_in.at[m], pm_send.at[m], pm_recv.at[m], {"tile": mirror})

    def send_mirror(m):
        mirror_out[m] = jnp.zeros((8, 128), F32)
        for n in range(2):
            (a, b), _ = MIRRORED[2 * m + n]
            mirror_out[m, n : n + 1, :] = leaving_row(a, b, True)
        p_mirror(m).start()

    send_mirror(0)

    def gather_p(hub):
        n = 0 if hub else 1
        return remote(hub_out.at[n], gath_p.at[t], ph_send.at[n], pgath_recv.at[t], {"tile": hub})

    up, down = t % 8, (LAST - t) % 8
    for n, hub in enumerate((LAST, 0)):
        panel = 1 if hub else 3
        hub_out[n] = jnp.zeros((8, 128), F32)
        hub_out[n, 0:1, :] = pltpu.roll(leaving_row(panel, 0, bool(hub)), 16 * (down if hub else up), 1)
        hub_out[n, 1:2, :] = pltpu.roll(leaving_row(panel, 1, not hub), 16 * (up if hub else down), 1)

        @pl.when(t != hub)
        def _():
            gather_p(hub).start()

        @pl.when(t == hub)
        def _():
            gath_p[t] = hub_out[n]

    def scatter_p(u, hub):
        n = 0 if hub else 1
        return remote(scat_p.at[u // 8], hub_in.at[n], ps_send.at[u], ps_recv.at[n], {"tile": u})

    @pl.when(is_hub)
    def _():
        rows = prow[jnp.where(is_last, 1, 0)]
        for block_at in range(4):
            ahead = rows[:, 128 * block_at : 128 * block_at + 128]
            behind = rows[:, 128 * (3 - block_at) : 128 * (3 - block_at) + 128]
            w = jnp.where(is_last, behind, ahead)
            e = jnp.where(is_last, ahead, behind)
            scat_p[block_at] = jnp.zeros((8, 128), F32)
            scat_p[block_at, 0:1, :] = w[5:6]
            scat_p[block_at, 1:2, :] = e[4:5]

        def one(u, c):
            @pl.when(jnp.logical_and(u != t, is_last))
            def _():
                scatter_p(u, LAST).start()

            @pl.when(jnp.logical_and(u != t, is_first))
            def _():
                scatter_p(u, 0).start()

            return c

        lax.fori_loop(0, TILES, one, 0)

        @pl.when(is_last)
        def _():
            hub_in[0] = scat_p[t // 8]

        @pl.when(is_first)
        def _():
            hub_in[1] = scat_p[t // 8]

    lax.fori_loop(4, PANELS, inner, 0)
    lax.fori_loop(3, PANELS, lambda n, c: fold_leaving(n * (n // 4), c), 0)
    send_mirror(1)

    cell = iota((ROWS, CELLS), 1)

    def fold_part(p, c):
        mine = (acc_s[p, 2:18] + acc_s[p, 1:17]) - (acc_n[p, 0:16] + acc_n[p, 1:17])
        to_e, to_w = sum_e[p], sum_w[p]
        moved_e = jnp.where(cell == 0, 0.0, pltpu.roll(to_e, 1, 1))
        moved_w = jnp.where(cell == CELLS - 1, 0.0, pltpu.roll(to_w, CELLS - 1, 1))
        part[p] = fold(fold_rows, mine.reshape(8 * ROWS, CELLS)) + ((to_e - to_w) + (moved_e - moved_w))
        return c

    lax.fori_loop(0, PANELS, fold_part, 0)

    def add_column(p, side, column):
        if side:
            at, lane = CELLS - 128, 127
        else:
            at, lane = 0, 0
        spread_out = jnp.broadcast_to(column, (16, 128))
        part[p, :, at : at + 128] += jnp.where(lane16 == lane, spread_out, 0.0)

    add_column(5, 1, leaving_column(0, 0))
    add_column(4, 0, leaving_column(0, 1))
    add_column(0, 1, leaving_column(4, 0))
    add_column(0, 0, leaving_column(5, 1))

    def row_to_column(row, base, reverse):
        spot = base + (15 - row16 if reverse else row16)
        spread_out = jnp.broadcast_to(row, (16, 128))
        return jnp.sum(jnp.where(lane16 == spot, spread_out, 0.0), axis=1, keepdims=True)

    p_south.wait_recv()
    p_north.wait_recv()
    from_north = precv[0]
    from_south = precv[1]
    pad = jnp.zeros((4, CELLS), F32)
    from_north = jnp.where(is_first, jnp.concatenate([from_north[3:4], from_north[0:3], pad], 0), from_north)
    from_south = jnp.where(is_last, jnp.concatenate([from_south[1:4], from_south[0:1], pad], 0), from_south)
    for p in range(PANELS):
        part[p, 0:1, :] += from_north[p : p + 1]
        part[p, ROWS - 1 : ROWS, :] += from_south[p : p + 1]

    def from_mirror(m):
        p_mirror(m).wait_recv()
        for n in range(2):
            _, (a, b) = MIRRORED[2 * m + n]
            add_column(a, b, row_to_column(mirror_in[m, n : n + 1, :], 0, False))

    from_mirror(0)

    @pl.when(is_hub)
    def _():
        def wait_one(u, c):
            @pl.when(u != t)
            def _():
                remote(hub_out.at[0], gath_p.at[u], ph_send.at[0], pgath_recv.at[u], {"tile": u}).wait_recv()
            return c

        lax.fori_loop(0, TILES, wait_one, 0)
        row_at = jnp.where(is_last, ROWS - 1, 0)
        for block_at in range(4):
            cols = slice(128 * block_at, 128 * block_at + 128)
            for side in range(2):
                total = jnp.zeros((8, 128), F32)
                for k in range(8):
                    seg = 8 * block_at + k
                    total = total + gath_p[seg_e(seg) if side else seg_w(seg)]
                row = jnp.broadcast_to(total[side : side + 1, :], (16, 128))
                part[5 - side, :, cols] += jnp.where(row16 == row_at, row, 0.0)

    GROUPS = ((0, 4, 5), (1, 2, 3))

    def each_peer(fn):
        def one(d, c):
            fn((s + d) % SAMPS)
            return c

        lax.fori_loop(1, SAMPS, one, 0)

    def reduce_to(m, peer):
        return remote(rs_in.at[m, peer], ag.at[m, s], rs_send.at[m, peer], rs_recv.at[m, s], {"samp": peer})

    def reduce_from(m, peer):
        return remote(rs_in.at[m, peer], ag.at[m, peer], rs_send.at[m, peer], rs_recv.at[m, peer], {"samp": peer})

    def share_with(m, peer):
        return remote(done.at[m, s], done.at[m, s], ag_send.at[m, peer], ag_recv.at[m, s], {"samp": peer})

    def share_from(m, peer):
        return remote(done.at[m, peer], done.at[m, peer], ag_send.at[m, peer], ag_recv.at[m, peer], {"samp": peer})

    def reduce_start(m):
        for n in range(SAMPS):
            h, k = n // 4, n % 4
            for j, p in enumerate(GROUPS[m]):
                rs_in[m, n, j] = part[p, 8 * h : 8 * h + 8, 128 * k : 128 * k + 128]
        each_peer(lambda peer: reduce_to(m, peer).start())
        ag[m, s] = rs_in[m, s]

    def reduce_end(m):
        each_peer(lambda peer: reduce_from(m, peer).wait_recv())
        total = ag[m, 0]
        for n in range(1, SAMPS):
            total = total + ag[m, n]
        done[m, s] = total * (0.005 / SAMPS)
        each_peer(lambda peer: share_with(m, peer).start())

    reduce_start(0)

    @pl.when(t != LAST)
    def _():
        scatter_p(LAST, LAST).wait_recv()

    @pl.when(t != 0)
    def _():
        scatter_p(0, 0).wait_recv()

    add_column(1, 0, row_to_column(hub_in[0, 0:1, :], 16 * down, True))
    add_column(1, 1, row_to_column(hub_in[0, 1:2, :], 16 * up, False))
    add_column(3, 0, row_to_column(hub_in[1, 0:1, :], 16 * up, False))
    add_column(3, 1, row_to_column(hub_in[1, 1:2, :], 16 * down, True))
    from_mirror(1)
    reduce_start(1)
    reduce_end(0)
    reduce_end(1)
    for m in range(2):
        each_peer(lambda peer: share_from(m, peer).wait_recv())
        for n in range(SAMPS):
            h, k = n // 4, n % 4
            for j, p in enumerate(GROUPS[m]):
                out_ref[p, 8 * h : 8 * h + 8, 128 * k : 128 * k + 128] = done[m, n, j]

    for m in range(2):
        each_peer(lambda peer: reduce_to(m, peer).wait_send())
        each_peer(lambda peer: share_with(m, peer).wait_send())
        p_mirror(m).wait_send()

    def rows_left(p, c):
        @pl.when(south_goes(p))
        def _():
            row_south(p).wait_send()

        @pl.when(north_goes(p))
        def _():
            row_north(p).wait_send()

        return c

    lax.fori_loop(0, PANELS, rows_left, 0)
    for n in range(4):
        mirrored(n).wait_send()
    p_south.wait_send()
    p_north.wait_send()
    for hub in (LAST, 0):
        @pl.when(t != hub)
        def _():
            gather_to(hub).wait_send()
            gather_p(hub).wait_send()

    @pl.when(is_hub)
    def _():
        def one(u, c):
            @pl.when(u != t)
            def _():
                scatter_to(u, 1).wait_send()
                scatter_p(u, LAST).wait_send()
            return c

        lax.fori_loop(0, TILES, one, 0)


def body(bathymetry, initial_state, patterns, pattern_index, coupling, final_weights):
    vmem = pl.BlockSpec(memory_space=pltpu.VMEM)
    hbm = pl.BlockSpec(memory_space=pl.ANY)
    tile = (8, 128)
    dma = pltpu.SemaphoreType.DMA
    return pl.pallas_call(
        kernel,
        out_shape=jax.ShapeDtypeStruct((PANELS, ROWS, CELLS), F32),
        in_specs=[hbm, hbm, hbm, vmem, vmem, hbm],
        out_specs=vmem,
        scratch_shapes=[
            pltpu.VMEM((PANELS, LAYERS, ROWS, CELLS), F32),
            pltpu.VMEM((PANELS, LAYERS, ROWS, CELLS), F32),
            pltpu.VMEM((4, PANELS, ROWS, CELLS), BF16),
            pltpu.VMEM((PANELS, ROWS, CELLS), F32),
            pltpu.VMEM((256, 768), BF16),
            pltpu.VMEM((256, 768), BF16),
            pltpu.VMEM((256, 576), BF16),
            pltpu.VMEM((PANELS, ROWS + 2, 40, CELLS), F32),
            pltpu.VMEM((PANELS, ROWS, LAYERS, CELLS), F32),
            pltpu.VMEM((PANELS, ROWS, 8, CELLS), F32),
            pltpu.VMEM((PANELS, ROWS, 8, CELLS), F32),
            pltpu.VMEM((PANELS, ROWS + 2, 8, CELLS), F32),
            pltpu.VMEM((PANELS, ROWS + 2, 8, CELLS), F32),
            pltpu.VMEM((PANELS, ROWS, CELLS), F32),
            pltpu.VMEM((PANELS, ROWS, CELLS), F32),
            pltpu.VMEM((PANELS, 2) + tile, F32),
            pltpu.VMEM((PANELS, 2) + tile, F32),
            pltpu.VMEM((TILES, 2) + tile, F32),
            pltpu.VMEM((TILES, 2) + tile, F32),
            pltpu.VMEM((2, 8, CELLS), F32),
            pltpu.VMEM((2, 8, CELLS), F32),
            pltpu.VMEM((2,) + tile, F32),
            pltpu.VMEM((2,) + tile, F32),
            pltpu.VMEM((2,) + tile, F32),
            pltpu.VMEM((TILES,) + tile, F32),
            pltpu.VMEM((4,) + tile, F32),
            pltpu.VMEM((2,) + tile, F32),
            pltpu.VMEM((PANELS, ROWS, CELLS), F32),
            pltpu.VMEM((2, SAMPS, 3) + tile, F32),
            pltpu.VMEM((2, SAMPS, 3) + tile, F32),
            pltpu.VMEM((2, SAMPS, 3) + tile, F32),
            dma((PANELS,)), dma((PANELS,)), dma((2,)),
            dma((2, PANELS)), dma((2, PANELS)),
            dma((2,)), dma((TILES,)), dma((4,)), dma((4,)),
            dma((TILES,)), dma((2,)),
            dma((2,)), dma((2,)), dma((2,)), dma((2,)),
            dma((2,)), dma((TILES,)), dma((TILES,)), dma((2,)),
            dma((2, SAMPS)), dma((2, SAMPS)), dma((2, SAMPS)), dma((2, SAMPS)),
        ],
        compiler_params=pltpu.CompilerParams(
            collective_id=0, has_side_effects=True, vmem_limit_bytes=56 * 1024 * 1024
        ),
        cost_estimate=pl.CostEstimate(flops=200_000_000, bytes_accessed=7_000_000, transcendentals=0),
    )(bathymetry, initial_state, patterns, pattern_index, coupling, final_weights)


def solution(mesh):
    in_specs = (
        P(None, "tile", None),
        P(None, None, "tile", None),
        P(None, None, "tile", None),
        P("samp", None),
        P(),
        P("samp", None, None, "tile", None),
    )
    out_specs = P(None, "tile", None)
    return jax.shard_map(body, mesh=mesh, in_specs=in_specs, out_specs=out_specs, check_vma=False)
```

```python
import jax
import jax.numpy as jnp
from jax import lax
from jax.experimental import pallas as pl
from jax.experimental.pallas import tpu as pltpu
from jax.sharding import PartitionSpec as P

F32, BF16 = jnp.float32, jnp.bfloat16
MESH = pl.DeviceIdType.MESH
TILES, SAMPS, ROWS, CELLS, LAYERS, PANELS = 32, 8, 16, 512, 16, 6
LAST = TILES - 1


def split(x):
    high = x.astype(BF16)
    return high, (x - high.astype(F32)).astype(BF16)


def iota(shape, axis):
    return lax.broadcasted_iota(jnp.int32, shape, axis)


def dot(a, b):
    return jnp.dot(a, b, preferred_element_type=F32)


def kernel(
    depth_hbm, state_hbm, pattern_hbm, index_ref, coupling_ref, weight_hbm, out_ref,
    xs, ws, ps, bs, kz, kv, kq, field, qf, acc_e, acc_w, acc_s, acc_n, sum_e, sum_w, pk, colh, gath, scat, prow, precv,
    mirror_out, mirror_in, hub_out, gath_p, scat_p, hub_in, part, rs_in, ag, done, late_in, late_ag, late_done, direct,
    load_x, load_w, load_pb, row_send, row_recv, hub_send, gath_recv, mir_send, mir_recv,
    scat_send, scat_recv, p_send, p_recv, pm_send, pm_recv, ph_send, pgath_recv, ps_send, ps_recv,
    rs_send, rs_recv, ag_send, ag_recv,
):
    t = lax.axis_index("tile")
    s = lax.axis_index("samp")
    left, right, mirror = (t + LAST) % TILES, (t + 1) % TILES, LAST - t
    is_first, is_last = t == 0, t == LAST
    is_hub = jnp.logical_or(is_first, is_last)
    at_end = t // LAST
    at_start = mirror // LAST

    def load(p):
        return (
            pltpu.make_async_copy(state_hbm.at[:, p], xs.at[p], load_x.at[p]),
            pltpu.make_async_copy(weight_hbm.at[0, :, p], ws.at[p], load_w.at[p]),
        )

    load_p = pltpu.make_async_copy(pattern_hbm, ps, load_pb.at[0])
    load_b = pltpu.make_async_copy(depth_hbm, bs, load_pb.at[1])
    for step in range(PANELS):
        for copy in load(PANELS - 1 - step):
            copy.start()
        if step == 0:
            load_p.start()
            load_b.start()

    barrier = pltpu.get_barrier_semaphore()

    def greet(device):
        pl.semaphore_signal(barrier, inc=1, device_id=device, device_id_type=MESH)

    def tell_tile(u, c):
        @pl.when(u != t)
        def _():
            greet({"tile": u})
        return c

    lax.fori_loop(0, TILES, tell_tile, 0)

    def tell_samp(u, c):
        @pl.when(u != s)
        def _():
            greet({"samp": u})
        return c

    lax.fori_loop(0, SAMPS, tell_samp, 0)

    mixing = coupling_ref[...] + jnp.where(iota((16, 16), 0) == iota((16, 16), 1), 1.0, 0.0)
    to_layer = (iota((256, 16), 0) % 16 == iota((256, 16), 1)).astype(BF16)
    from_layer = (iota((16, 256), 0) == iota((16, 256), 1) // 16).astype(BF16)
    same_row = iota((256, 256), 0) // 16 == iota((256, 256), 1) % 16

    def spread(matrix):
        tall = dot(to_layer, matrix).astype(BF16)
        return jnp.where(same_row, dot(tall, from_layer), 0.0).astype(BF16)

    for target, matrix in ((kz, mixing), (kv, mixing.T)):
        high, low = split(matrix)
        spread_high = spread(high)
        target[:, 0:256] = spread_high
        target[:, 256:512] = spread(low)
        target[:, 512:768] = spread_high
    thirty = jnp.where(
        jnp.logical_and(same_row, iota((256, 256), 0) % 16 == iota((256, 256), 1) // 16), 30.0, 0.0
    ).astype(BF16)
    kq[:, 0:256] = thirty
    kq[:, 256:512] = thirty
    chosen = (iota((4, 16), 0) == jnp.broadcast_to(index_ref[...], (4, 16))).astype(F32)
    tall = lax.dot_general(
        to_layer, chosen.astype(BF16), (((1,), (1,)), ((), ())), preferred_element_type=F32
    ).astype(BF16)
    from_pattern = (iota((4, 64), 0) == iota((4, 64), 1) // 16).astype(BF16)
    kq[:, 512:576] = jnp.where(
        iota((256, 64), 0) // 16 == iota((256, 64), 1) % 16, dot(tall, from_pattern), 0.0
    ).astype(BF16)

    acc_s[:, 1] = jnp.zeros((PANELS, 8, CELLS), F32)
    acc_n[:, 16] = jnp.zeros((PANELS, 8, CELLS), F32)
    lanes = iota((8, 128), 1)

    def remote(src, dst, send, recv, device):
        return pltpu.make_async_remote_copy(
            src_ref=src, dst_ref=dst, send_sem=send, recv_sem=recv,
            device_id=device, device_id_type=MESH,
        )

    def row_south(p):
        to = p + jnp.where(p < 4, at_end * ((p + 1) % 4 - p), 0)
        return remote(field.at[p, 16], field.at[to, 0], row_send.at[0, p], row_recv.at[0, to], {"tile": right})

    def row_north(p):
        to = p + jnp.where(p < 4, at_start * ((p + 3) % 4 - p), 0)
        return remote(field.at[p, 1], field.at[to, 17], row_send.at[1, p], row_recv.at[1, to], {"tile": left})

    def came_from_left(p):
        return remote(field.at[p, 16], field.at[p, 0], row_send.at[0, p], row_recv.at[0, p], {"tile": right})

    def came_from_right(p):
        return remote(field.at[p, 1], field.at[p, 17], row_send.at[1, p], row_recv.at[1, p], {"tile": left})

    def south_goes(p):
        return jnp.logical_or(p < 4, jnp.logical_not(is_last))

    def north_goes(p):
        return jnp.logical_or(p < 4, jnp.logical_not(is_first))

    def gather_to(hub):
        panel = 1 if hub else 3
        return remote(pk.at[panel], gath.at[t], hub_send.at[panel // 2], gath_recv.at[t], {"tile": hub})

    MIRRORED = (((2, 0), (5, 0)), ((2, 1), (4, 1)), ((5, 0), (2, 0)), ((4, 1), (2, 1)))

    def mirrored(n):
        (a, b), (c, d) = MIRRORED[n]
        return remote(pk.at[a, b], colh.at[c, d], mir_send.at[n], mir_recv.at[n], {"tile": mirror})

    def scatter_to(u, panel):
        return remote(scat.at[u], colh.at[panel], scat_send.at[u], scat_recv.at[panel // 2], {"tile": u})

    def seg_w(u):
        return jnp.where(is_last, LAST - u, u)

    def seg_e(u):
        return jnp.where(is_last, u, LAST - u)

    def make_scatter():
        slot = jnp.where(is_last, 16, 1)

        def one(u, c):
            for side in range(2):
                seg = seg_e(u) if side else seg_w(u)
                block, place = seg // 8, seg % 8
                out = jnp.zeros((8, 128), F32)
                for g in range(5):
                    x = field[5 - side, slot, pl.ds(8 * g, 8), pl.ds(pl.multiple_of(block * 128, 128), 128)]
                    x = pltpu.roll(x, (16 * g - 16 * place + 128) % 128, 1)
                    out = jnp.where(lanes // 16 == g, x, out)
                scat[u, side] = out

            @pl.when(jnp.logical_and(u != t, is_last))
            def _():
                scatter_to(u, 1).start()

            @pl.when(jnp.logical_and(u != t, is_first))
            def _():
                scatter_to(u, 3).start()

            return c

        lax.fori_loop(0, TILES, one, 0)

        @pl.when(is_last)
        def _():
            colh[1] = scat[t]

        @pl.when(is_first)
        def _():
            colh[3] = scat[t]

    def mix(step, c):
        p = PANELS - 1 - step
        for copy in load(p):
            copy.wait()
        xh, xl = split(xs[p].reshape(256, CELLS))
        z = dot(kz[...], jnp.concatenate([xh, xh, xl], 0))
        field[p, 1:17, 0:16, :] = z.reshape(ROWS, 16, CELLS)
        pat = ps[:, p].reshape(64, CELLS)
        q = dot(kq[...], jnp.concatenate([xh, xl, pat], 0))
        qf[p] = q.reshape(ROWS, 16, CELLS)
        wh, wl = split(ws[p].reshape(256, CELLS))
        v = dot(kv[...], jnp.concatenate([wh, wh, wl], 0))
        field[p, 1:17, 16:32, :] = v.reshape(ROWS, 16, CELLS)
        for i in range(ROWS):
            field[p, 1 + i, 32:40, :] = jnp.broadcast_to(0.5 * bs[p, i : i + 1, :], (8, CELLS))

        @pl.when(step == 0)
        def _():
            pl.semaphore_wait(barrier, TILES - 1 + SAMPS - 1)

        @pl.when(south_goes(p))
        def _():
            row_south(p).start()

        @pl.when(north_goes(p))
        def _():
            row_north(p).start()

        for side in range(2):
            if side == 0:
                rev = jnp.where(jnp.logical_or(p == 1, jnp.logical_or(p == 2, p == 5)), 1, 0)
            else:
                rev = jnp.where(jnp.logical_and(p >= 2, p <= 4), 1, 0)
            out = jnp.zeros((8, 128), F32)
            for i in range(ROWS):
                for g in range(5):
                    if side == 0:
                        x = field[p, 1 + i, 8 * g : 8 * g + 8, 0:128][:, 0:1]
                    else:
                        x = field[p, 1 + i, 8 * g : 8 * g + 8, CELLS - 128 : CELLS][:, 127:128]
                    spot = 16 * g + i + rev * (15 - 2 * i)
                    out = jnp.where(lanes == spot, jnp.broadcast_to(x, (8, 128)), out)
            pk[p, side] = out

        for at, hub in ((4, LAST), (2, 0)):
            @pl.when(jnp.logical_and(step == at, t != hub))
            def _():
                gather_to(hub).start()

            @pl.when(jnp.logical_and(step == at, t == hub))
            def _():
                gath[t] = pk[1 if hub else 3]

        @pl.when(jnp.logical_and(step == 1, is_hub))
        def _():
            make_scatter()

        @pl.when(step == 3)
        def _():
            for n in range(4):
                mirrored(n).start()

        return c

    load_p.wait()
    load_b.wait()
    lax.fori_loop(0, PANELS, mix, 0)

    colh[0, 0] = pk[5, 1]
    colh[0, 1] = pk[4, 0]
    colh[4, 0] = pk[0, 1]
    colh[5, 1] = pk[0, 0]

    first_lane, last_lane = lanes == 0, lanes == 127

    def block(g, p, slot, k):
        return field[p, slot, 8 * g : 8 * g + 8, 128 * k : 128 * k + 128]

    def stencil_row(p, i):
        slot = i + 1
        west, east = colh[p, 0], colh[p, 1]

        def sides(g):
            x = [block(g, p, slot, k) for k in range(4)]
            r = [pltpu.roll(y, 127, 1) for y in x] + [pltpu.roll(east, (127 - 16 * g - i) % 128, 1)]
            l = [pltpu.roll(west, (128 - 16 * g - i) % 128, 1)] + [pltpu.roll(y, 1, 1) for y in x]
            return (
                x,
                [jnp.where(last_lane, r[k + 1], r[k]) for k in range(4)],
                [jnp.where(first_lane, l[k], l[k + 1]) for k in range(4)],
            )

        every = [sides(g) for g in range(5)]
        for k in range(4):
            x, e, w = (v[k] for v in every[4])
            beta_e = x + e
            beta_w = x + w
            beta_s = x + block(4, p, slot + 1, k)
            beta_n = x + block(4, p, slot - 1, k)
            sums = None
            for half in range(2):
                both = []
                for g in (half, 2 + half):
                    x, e, w = (v[k] for v in every[g])
                    de = e - x
                    dw = x - w
                    ds = block(g, p, slot + 1, k) - x
                    dn = x - block(g, p, slot - 1, k)
                    lap = (beta_e * de - beta_w * dw) + (beta_s * ds - beta_n * dn)
                    both.append((lap, de, dw, ds, dn))
                (lz, *dz), (lv, *dv) = both
                q = lz + qf[p, i, 8 * half : 8 * half + 8, 128 * k : 128 * k + 128]
                terms = [x * q + y * lv for x, y in zip(dv, dz)]
                sums = terms if sums is None else [x + y for x, y in zip(sums, terms)]
            cols = slice(128 * k, 128 * k + 128)
            acc_e[p, i, :, cols] = sums[0]
            acc_w[p, i, :, cols] = sums[1]
            acc_s[p, slot + 1, :, cols] = sums[2]
            acc_n[p, slot - 1, :, cols] = sums[3]

    def stencil_rows(p, start, count):
        for r in range(count):
            stencil_row(p, start + r)

    def wait_columns():
        for n in range(4):
            mirrored(n).wait_recv()

        @pl.when(t != LAST)
        def _():
            scatter_to(LAST, 1).wait_recv()

        @pl.when(t != 0)
        def _():
            scatter_to(0, 3).wait_recv()

        turn(1, 0)
        turn(3, 1)

    def turn(p, side):
        x = colh[p, side]
        out = x
        for e in range(16):
            out = jnp.where(lanes % 16 == 15 - e, pltpu.roll(x, (15 - 2 * e) % 128, 1), out)
        colh[p, side] = out

    def inner(p, c):
        @pl.when(p == 1)
        def _():
            wait_columns()

        def seven(n, c):
            stencil_rows(p, 1 + 7 * n, 7)
            return c

        lax.fori_loop(0, 2, seven, 0)
        return c

    lax.fori_loop(0, 4, inner, 0)

    @pl.when(is_hub)
    def _():
        def wait_one(u, c):
            @pl.when(u != t)
            def _():
                remote(pk.at[1], gath.at[u], hub_send.at[0], gath_recv.at[u], {"tile": u}).wait_recv()
            return c

        lax.fori_loop(0, TILES, wait_one, 0)
        slot = jnp.where(is_last, 17, 0)

        def one(block, c):
            for side in range(2):
                for g in range(5):
                    out = jnp.zeros((8, 128), F32)
                    for k in range(8):
                        seg = 8 * block + k
                        u = seg_e(seg) if side else seg_w(seg)
                        x = pltpu.roll(gath[u, side], (16 * k - 16 * g + 128) % 128, 1)
                        out = jnp.where(lanes // 16 == k, x, out)
                    field[5 - side, slot, pl.ds(8 * g, 8), pl.ds(pl.multiple_of(block * 128, 128), 128)] = out
            return c

        lax.fori_loop(0, 4, one, 0)

    def outer(p, c):
        @pl.when(jnp.logical_or(p < 4, jnp.logical_not(is_first)))
        def _():
            came_from_left(p).wait_recv()

        @pl.when(jnp.logical_or(p < 4, jnp.logical_not(is_last)))
        def _():
            came_from_right(p).wait_recv()

        stencil_rows(p, 0, 1)
        stencil_rows(p, ROWS - 1, 1)
        return c

    lax.fori_loop(0, PANELS, outer, 0)

    def fold(matrix, x):
        high, low = split(x)
        return dot(matrix, high) + dot(matrix, low)

    fold_rows = (iota((ROWS, 8 * ROWS), 0) == iota((ROWS, 8 * ROWS), 1) // 8).astype(BF16)
    fold_panels = (iota((8, 8 * PANELS), 0) == iota((8, 8 * PANELS), 1) // 8).astype(BF16)
    lane16, row16 = iota((16, 128), 1), iota((16, 128), 0)

    prow[0] = -fold(fold_panels, acc_n[:, 0].reshape(8 * PANELS, CELLS))
    prow[1] = fold(fold_panels, acc_s[:, 17].reshape(8 * PANELS, CELLS))
    p_south = remote(prow.at[1], precv.at[0], p_send.at[0], p_recv.at[0], {"tile": right})
    p_north = remote(prow.at[0], precv.at[1], p_send.at[1], p_recv.at[1], {"tile": left})
    p_south.start()
    p_north.start()

    def fold_leaving(p, c):
        sum_e[p] = fold(fold_rows, acc_e[p].reshape(8 * ROWS, CELLS))
        sum_w[p] = fold(fold_rows, acc_w[p].reshape(8 * ROWS, CELLS))
        return c

    lax.fori_loop(0, 4, fold_leaving, 0)

    def leaving_column(p, side):
        return sum_e[p, :, CELLS - 128 :][:, 127:128] if side else -sum_w[p, :, 0:128][:, 0:1]

    def leaving_row(p, side, reverse):
        spot = 15 - row16 if reverse else row16
        column = jnp.broadcast_to(leaving_column(p, side), (16, 128))
        return jnp.sum(jnp.where(lane16 == spot, column, 0.0), axis=0, keepdims=True)

    def p_mirror(m):
        return remote(mirror_out.at[m], mirror_in.at[m], pm_send.at[m], pm_recv.at[m], {"tile": mirror})

    def send_mirror(m):
        mirror_out[m] = jnp.zeros((8, 128), F32)
        for n in range(2):
            (a, b), _ = MIRRORED[2 * m + n]
            mirror_out[m, n : n + 1, :] = leaving_row(a, b, True)
        p_mirror(m).start()

    send_mirror(0)

    def gather_p(hub):
        n = 0 if hub else 1
        return remote(hub_out.at[n], gath_p.at[t], ph_send.at[n], pgath_recv.at[t], {"tile": hub})

    up, down = t % 8, (LAST - t) % 8
    for n, hub in enumerate((LAST, 0)):
        panel = 1 if hub else 3
        hub_out[n] = jnp.zeros((8, 128), F32)
        hub_out[n, 0:1, :] = pltpu.roll(leaving_row(panel, 0, bool(hub)), 16 * (down if hub else up), 1)
        hub_out[n, 1:2, :] = pltpu.roll(leaving_row(panel, 1, not hub), 16 * (up if hub else down), 1)

        @pl.when(t != hub)
        def _():
            gather_p(hub).start()

        @pl.when(t == hub)
        def _():
            gath_p[t] = hub_out[n]

    def scatter_p(u, hub):
        n = 0 if hub else 1
        return remote(scat_p.at[u // 8], hub_in.at[n], ps_send.at[u], ps_recv.at[n], {"tile": u})

    @pl.when(is_hub)
    def _():
        rows = prow[jnp.where(is_last, 1, 0)]
        for block_at in range(4):
            ahead = rows[:, 128 * block_at : 128 * block_at + 128]
            behind = rows[:, 128 * (3 - block_at) : 128 * (3 - block_at) + 128]
            w = jnp.where(is_last, behind, ahead)
            e = jnp.where(is_last, ahead, behind)
            scat_p[block_at] = jnp.zeros((8, 128), F32)
            scat_p[block_at, 0:1, :] = w[5:6]
            scat_p[block_at, 1:2, :] = e[4:5]

        def one(u, c):
            @pl.when(jnp.logical_and(u != t, is_last))
            def _():
                scatter_p(u, LAST).start()

            @pl.when(jnp.logical_and(u != t, is_first))
            def _():
                scatter_p(u, 0).start()

            return c

        lax.fori_loop(0, TILES, one, 0)

        @pl.when(is_last)
        def _():
            hub_in[0] = scat_p[t // 8]

        @pl.when(is_first)
        def _():
            hub_in[1] = scat_p[t // 8]

    GROUPS = ((0, 1, 2, 3),)

    def each_peer(fn):
        def one(d, c):
            fn((s + d) % SAMPS)
            return c

        lax.fori_loop(1, SAMPS, one, 0)

    def reduce_to(m, peer):
        return remote(rs_in.at[m, peer], ag.at[m, s], rs_send.at[m, peer], rs_recv.at[m, s], {"samp": peer})

    def reduce_from(m, peer):
        return remote(rs_in.at[m, peer], ag.at[m, peer], rs_send.at[m, peer], rs_recv.at[m, peer], {"samp": peer})

    def share_with(m, peer):
        return remote(done.at[m, s], done.at[m, s], ag_send.at[m, peer], ag_recv.at[m, s], {"samp": peer})

    def share_from(m, peer):
        return remote(done.at[m, peer], done.at[m, peer], ag_send.at[m, peer], ag_recv.at[m, peer], {"samp": peer})

    def direct_to(peer):
        return remote(part.at[pl.ds(4, 2)], direct.at[s], rs_send.at[1, peer], rs_recv.at[1, s], {"samp": peer})

    def direct_from(peer):
        return remote(part.at[pl.ds(4, 2)], direct.at[peer], rs_send.at[1, peer], rs_recv.at[1, peer], {"samp": peer})

    def late_to(peer):
        return remote(late_in, late_ag.at[s], rs_send.at[2, peer], rs_recv.at[2, s], {"samp": peer})

    def late_from(peer):
        return remote(late_in, late_ag.at[peer], rs_send.at[2, peer], rs_recv.at[2, peer], {"samp": peer})

    def summed(parts):
        total = parts[0]
        for n in range(1, SAMPS):
            total = total + parts[n]
        return total * (0.005 / SAMPS)

    def reduce_start(m):
        for n in range(SAMPS):
            h, k = n // 4, n % 4
            for j, p in enumerate(GROUPS[m]):
                rs_in[m, n, j] = part[p, 8 * h : 8 * h + 8, 128 * k : 128 * k + 128]
        each_peer(lambda peer: reduce_to(m, peer).start())
        ag[m, s] = rs_in[m, s]

    def reduce_end(m):
        each_peer(lambda peer: reduce_from(m, peer).wait_recv())
        done[m, s] = summed([ag[m, n] for n in range(SAMPS)])
        each_peer(lambda peer: share_with(m, peer).start())

    def share_end(m):
        each_peer(lambda peer: share_from(m, peer).wait_recv())
        for n in range(SAMPS):
            h, k = n // 4, n % 4
            for j, p in enumerate(GROUPS[m]):
                out_ref[p, 8 * h : 8 * h + 8, 128 * k : 128 * k + 128] = done[m, n, j]

    cell = iota((ROWS, CELLS), 1)

    def fold_part(p, c):
        mine = (acc_s[p, 2:18] + acc_s[p, 1:17]) - (acc_n[p, 0:16] + acc_n[p, 1:17])
        to_e, to_w = sum_e[p], sum_w[p]
        moved_e = jnp.where(cell == 0, 0.0, pltpu.roll(to_e, 1, 1))
        moved_w = jnp.where(cell == CELLS - 1, 0.0, pltpu.roll(to_w, CELLS - 1, 1))
        part[p] = fold(fold_rows, mine.reshape(8 * ROWS, CELLS)) + ((to_e - to_w) + (moved_e - moved_w))
        return c

    lax.fori_loop(0, 4, fold_part, 0)
    reduce_start(0)

    lax.fori_loop(4, PANELS, inner, 0)
    lax.fori_loop(4, PANELS, fold_leaving, 0)
    send_mirror(1)
    lax.fori_loop(4, PANELS, fold_part, 0)

    def add_column(target, p, side, column):
        at, lane = (CELLS - 128, 127) if side else (0, 0)
        spread_out = jnp.broadcast_to(column, (16, 128))
        target[p, :, at : at + 128] += jnp.where(lane16 == lane, spread_out, 0.0)

    add_column(part, 5, 1, leaving_column(0, 0))
    add_column(part, 4, 0, leaving_column(0, 1))
    each_peer(lambda peer: direct_to(peer).start())
    direct[s] = part[4:6]
    reduce_end(0)

    def row_to_column(row, base, reverse):
        spot = base + (15 - row16 if reverse else row16)
        spread_out = jnp.broadcast_to(row, (16, 128))
        return jnp.sum(jnp.where(lane16 == spot, spread_out, 0.0), axis=1, keepdims=True)

    def placed(p, side, column):
        return jnp.where(lane16 == 2 * p + side, jnp.broadcast_to(column, (16, 128)), 0.0)

    p_south.wait_recv()
    p_north.wait_recv()
    from_north = precv[0]
    from_south = precv[1]
    pad = jnp.zeros((4, CELLS), F32)
    from_north = jnp.where(is_first, jnp.concatenate([from_north[3:4], from_north[0:3], pad], 0), from_north)
    from_south = jnp.where(is_last, jnp.concatenate([from_south[1:4], from_south[0:1], pad], 0), from_south)
    for n in range(SAMPS):
        h, k = n // 4, n % 4
        late_in[n] = (from_south if h else from_north)[:, 128 * k : 128 * k + 128]

    @pl.when(is_hub)
    def _():
        def wait_one(u, c):
            @pl.when(u != t)
            def _():
                remote(hub_out.at[0], gath_p.at[u], ph_send.at[0], pgath_recv.at[u], {"tile": u}).wait_recv()
            return c

        lax.fori_loop(0, TILES, wait_one, 0)
        panel_row = iota((8, 128), 0)
        first_chunk = 4 * at_end
        for block_at in range(4):
            for side in range(2):
                total = jnp.zeros((8, 128), F32)
                for k in range(8):
                    seg = 8 * block_at + k
                    total = total + gath_p[seg_e(seg) if side else seg_w(seg)]
                row = jnp.broadcast_to(total[side : side + 1, :], (8, 128))
                late_in[first_chunk + block_at] += jnp.where(panel_row == 5 - side, row, 0.0)

    @pl.when(t != LAST)
    def _():
        scatter_p(LAST, LAST).wait_recv()

    @pl.when(t != 0)
    def _():
        scatter_p(0, 0).wait_recv()

    columns = placed(0, 1, leaving_column(4, 0)) + placed(0, 0, leaving_column(5, 1))
    columns = columns + placed(1, 0, row_to_column(hub_in[0, 0:1, :], 16 * down, True))
    columns = columns + placed(1, 1, row_to_column(hub_in[0, 1:2, :], 16 * up, False))
    columns = columns + placed(3, 0, row_to_column(hub_in[1, 0:1, :], 16 * up, False))
    columns = columns + placed(3, 1, row_to_column(hub_in[1, 1:2, :], 16 * down, True))
    for m in range(2):
        p_mirror(m).wait_recv()
        for n in range(2):
            _, (a, b) = MIRRORED[2 * m + n]
            columns = columns + placed(a, b, row_to_column(mirror_in[m, n : n + 1, :], 0, False))
    late_in[8] = columns[0:8]
    late_in[9] = columns[8:16]
    each_peer(lambda peer: late_to(peer).start())
    late_ag[s] = late_in[...]
    each_peer(lambda peer: direct_from(peer).wait_recv())
    out_ref[4:6] = summed([direct[n] for n in range(SAMPS)])
    share_end(0)
    each_peer(lambda peer: late_from(peer).wait_recv())
    late_done[...] = summed([late_ag[n] for n in range(SAMPS)])
    for n in range(SAMPS):
        h, k = n // 4, n % 4
        for p in range(PANELS):
            row = slice(15, 16) if h else slice(0, 1)
            out_ref[p, row, 128 * k : 128 * k + 128] += late_done[n, p : p + 1, :]
    columns = jnp.concatenate([late_done[8], late_done[9]], 0)
    for p, side in ((0, 0), (0, 1), (1, 0), (1, 1), (3, 0), (3, 1), (2, 0), (2, 1), (5, 0), (4, 1)):
        add_column(out_ref, p, side, columns[:, 2 * p + side : 2 * p + side + 1])

    for copy_to in (lambda peer: reduce_to(0, peer), lambda peer: share_with(0, peer), direct_to, late_to):
        each_peer(lambda peer: copy_to(peer).wait_send())
    p_mirror(0).wait_send()
    p_mirror(1).wait_send()

    def rows_left(p, c):
        @pl.when(south_goes(p))
        def _():
            row_south(p).wait_send()

        @pl.when(north_goes(p))
        def _():
            row_north(p).wait_send()

        return c

    lax.fori_loop(0, PANELS, rows_left, 0)
    for n in range(4):
        mirrored(n).wait_send()
    p_south.wait_send()
    p_north.wait_send()
    for hub in (LAST, 0):
        @pl.when(t != hub)
        def _():
            gather_to(hub).wait_send()
            gather_p(hub).wait_send()

    @pl.when(is_hub)
    def _():
        def one(u, c):
            @pl.when(u != t)
            def _():
                scatter_to(u, 1).wait_send()
                scatter_p(u, LAST).wait_send()
            return c

        lax.fori_loop(0, TILES, one, 0)


def body(bathymetry, initial_state, patterns, pattern_index, coupling, final_weights):
    vmem = pl.BlockSpec(memory_space=pltpu.VMEM)
    hbm = pl.BlockSpec(memory_space=pl.ANY)
    tile = (8, 128)
    dma = pltpu.SemaphoreType.DMA
    return pl.pallas_call(
        kernel,
        out_shape=jax.ShapeDtypeStruct((PANELS, ROWS, CELLS), F32),
        in_specs=[hbm, hbm, hbm, vmem, vmem, hbm],
        out_specs=vmem,
        scratch_shapes=[
            pltpu.VMEM((PANELS, LAYERS, ROWS, CELLS), F32),
            pltpu.VMEM((PANELS, LAYERS, ROWS, CELLS), F32),
            pltpu.VMEM((4, PANELS, ROWS, CELLS), BF16),
            pltpu.VMEM((PANELS, ROWS, CELLS), F32),
            pltpu.VMEM((256, 768), BF16),
            pltpu.VMEM((256, 768), BF16),
            pltpu.VMEM((256, 576), BF16),
            pltpu.VMEM((PANELS, ROWS + 2, 40, CELLS), F32),
            pltpu.VMEM((PANELS, ROWS, LAYERS, CELLS), F32),
            pltpu.VMEM((PANELS, ROWS, 8, CELLS), F32),
            pltpu.VMEM((PANELS, ROWS, 8, CELLS), F32),
            pltpu.VMEM((PANELS, ROWS + 2, 8, CELLS), F32),
            pltpu.VMEM((PANELS, ROWS + 2, 8, CELLS), F32),
            pltpu.VMEM((PANELS, ROWS, CELLS), F32),
            pltpu.VMEM((PANELS, ROWS, CELLS), F32),
            pltpu.VMEM((PANELS, 2) + tile, F32),
            pltpu.VMEM((PANELS, 2) + tile, F32),
            pltpu.VMEM((TILES, 2) + tile, F32),
            pltpu.VMEM((TILES, 2) + tile, F32),
            pltpu.VMEM((2, 8, CELLS), F32),
            pltpu.VMEM((2, 8, CELLS), F32),
            pltpu.VMEM((2,) + tile, F32),
            pltpu.VMEM((2,) + tile, F32),
            pltpu.VMEM((2,) + tile, F32),
            pltpu.VMEM((TILES,) + tile, F32),
            pltpu.VMEM((4,) + tile, F32),
            pltpu.VMEM((2,) + tile, F32),
            pltpu.VMEM((PANELS, ROWS, CELLS), F32),
            pltpu.VMEM((1, SAMPS, 4) + tile, F32),
            pltpu.VMEM((1, SAMPS, 4) + tile, F32),
            pltpu.VMEM((1, SAMPS, 4) + tile, F32),
            pltpu.VMEM((10,) + tile, F32),
            pltpu.VMEM((SAMPS, 10) + tile, F32),
            pltpu.VMEM((10,) + tile, F32),
            pltpu.VMEM((SAMPS, 2, ROWS, CELLS), F32),
            dma((PANELS,)), dma((PANELS,)), dma((2,)),
            dma((2, PANELS)), dma((2, PANELS)),
            dma((2,)), dma((TILES,)), dma((4,)), dma((4,)),
            dma((TILES,)), dma((2,)),
            dma((2,)), dma((2,)), dma((2,)), dma((2,)),
            dma((2,)), dma((TILES,)), dma((TILES,)), dma((2,)),
            dma((3, SAMPS)), dma((3, SAMPS)), dma((1, SAMPS)), dma((1, SAMPS)),
        ],
        compiler_params=pltpu.CompilerParams(
            collective_id=0, has_side_effects=True, vmem_limit_bytes=56 * 1024 * 1024
        ),
        cost_estimate=pl.CostEstimate(flops=200_000_000, bytes_accessed=7_000_000, transcendentals=0),
    )(bathymetry, initial_state, patterns, pattern_index, coupling, final_weights)


def solution(mesh):
    in_specs = (
        P(None, "tile", None),
        P(None, None, "tile", None),
        P(None, None, "tile", None),
        P("samp", None),
        P(),
        P("samp", None, None, "tile", None),
    )
    out_specs = P(None, "tile", None)
    return jax.shard_map(body, mesh=mesh, in_specs=in_specs, out_specs=out_specs, check_vma=False)
```

```python
import jax
import jax.numpy as jnp
from jax import lax
from jax.experimental import pallas as pl
from jax.experimental.pallas import tpu as pltpu
from jax.sharding import PartitionSpec as P

F32, BF16 = jnp.float32, jnp.bfloat16
MESH = pl.DeviceIdType.MESH
TILES, SAMPS, ROWS, CELLS, LAYERS, PANELS = 32, 8, 16, 512, 16, 6
LAST = TILES - 1


def split(x):
    high = x.astype(BF16)
    return high, (x - high.astype(F32)).astype(BF16)


def iota(shape, axis):
    return lax.broadcasted_iota(jnp.int32, shape, axis)


def dot(a, b):
    return jnp.dot(a, b, preferred_element_type=F32)


def kernel(
    depth_hbm, state_hbm, pattern_hbm, index_hbm, coupling_hbm, weight_hbm, out_ref,
    index_ref, coupling_ref,
    xs, ws, ps, bs, kz, kv, kq, field, qf, acc_e, acc_w, acc_s, acc_n, sum_e, sum_w, pk, colh, gath, scat, prow, precv,
    mirror_out, mirror_in, hub_out, gath_p, scat_p, hub_in, part, rs_in, ag, done, late_in, late_ag, late_done, direct,
    load_x, load_w, load_pb, row_send, row_recv, hub_send, gath_recv, mir_send, mir_recv,
    scat_send, scat_recv, p_send, p_recv, pm_send, pm_recv, ph_send, pgath_recv, ps_send, ps_recv,
    rs_send, rs_recv, ag_send, ag_recv,
):
    t = lax.axis_index("tile")
    s = lax.axis_index("samp")
    left, right, mirror = (t + LAST) % TILES, (t + 1) % TILES, LAST - t
    is_first, is_last = t == 0, t == LAST
    is_hub = jnp.logical_or(is_first, is_last)
    at_end = t // LAST
    at_start = mirror // LAST

    def load(p):
        return (
            pltpu.make_async_copy(state_hbm.at[:, p], xs.at[p], load_x.at[p]),
            pltpu.make_async_copy(weight_hbm.at[0, :, p], ws.at[p], load_w.at[p]),
        )

    load_p = pltpu.make_async_copy(pattern_hbm, ps, load_pb.at[0])
    load_b = pltpu.make_async_copy(depth_hbm, bs, load_pb.at[1])
    load_i = pltpu.make_async_copy(index_hbm, index_ref, load_pb.at[2])
    load_c = pltpu.make_async_copy(coupling_hbm, coupling_ref, load_pb.at[3])
    load_c.start()
    load_i.start()
    for step in range(PANELS):
        for copy in load(PANELS - 1 - step):
            copy.start()
        if step == 0:
            load_p.start()
            load_b.start()

    barrier = pltpu.get_barrier_semaphore()

    def greet(device):
        pl.semaphore_signal(barrier, inc=1, device_id=device, device_id_type=MESH)

    for d in range(1, SAMPS):
        greet({"samp": (s + d) % SAMPS})
    for d in range(1, TILES):
        greet({"tile": (t + d) % TILES})

    load_c.wait()
    load_i.wait()
    mixing = coupling_ref[...] + jnp.where(iota((16, 16), 0) == iota((16, 16), 1), 1.0, 0.0)
    to_layer = (iota((256, 16), 0) % 16 == iota((256, 16), 1)).astype(BF16)
    from_layer = (iota((16, 256), 0) == iota((16, 256), 1) // 16).astype(BF16)
    same_row = iota((256, 256), 0) // 16 == iota((256, 256), 1) % 16

    def spread(matrix):
        tall = dot(to_layer, matrix).astype(BF16)
        return jnp.where(same_row, dot(tall, from_layer), 0.0).astype(BF16)

    for target, matrix in ((kz, mixing), (kv, mixing.T)):
        high, low = split(matrix)
        spread_high = spread(high)
        target[:, 0:256] = spread_high
        target[:, 256:512] = spread(low)
        target[:, 512:768] = spread_high
    thirty = jnp.where(
        jnp.logical_and(same_row, iota((256, 256), 0) % 16 == iota((256, 256), 1) // 16), 30.0, 0.0
    ).astype(BF16)
    kq[:, 0:256] = thirty
    kq[:, 256:512] = thirty
    chosen = (iota((4, 16), 0) == jnp.broadcast_to(index_ref[...], (4, 16))).astype(F32)
    tall = lax.dot_general(
        to_layer, chosen.astype(BF16), (((1,), (1,)), ((), ())), preferred_element_type=F32
    ).astype(BF16)
    from_pattern = (iota((4, 64), 0) == iota((4, 64), 1) // 16).astype(BF16)
    kq[:, 512:576] = jnp.where(
        iota((256, 64), 0) // 16 == iota((256, 64), 1) % 16, dot(tall, from_pattern), 0.0
    ).astype(BF16)

    acc_s[:, 1] = jnp.zeros((PANELS, 8, CELLS), F32)
    acc_n[:, 16] = jnp.zeros((PANELS, 8, CELLS), F32)
    lanes = iota((8, 128), 1)

    def remote(src, dst, send, recv, device):
        return pltpu.make_async_remote_copy(
            src_ref=src, dst_ref=dst, send_sem=send, recv_sem=recv,
            device_id=device, device_id_type=MESH,
        )

    def row_south(p):
        to = p + jnp.where(p < 4, at_end * ((p + 1) % 4 - p), 0)
        return remote(field.at[p, 16], field.at[to, 0], row_send.at[0, p], row_recv.at[0, to], {"tile": right})

    def row_north(p):
        to = p + jnp.where(p < 4, at_start * ((p + 3) % 4 - p), 0)
        return remote(field.at[p, 1], field.at[to, 17], row_send.at[1, p], row_recv.at[1, to], {"tile": left})

    def came_from_left(p):
        return remote(field.at[p, 16], field.at[p, 0], row_send.at[0, p], row_recv.at[0, p], {"tile": right})

    def came_from_right(p):
        return remote(field.at[p, 1], field.at[p, 17], row_send.at[1, p], row_recv.at[1, p], {"tile": left})

    def south_goes(p):
        return jnp.logical_or(p < 4, jnp.logical_not(is_last))

    def north_goes(p):
        return jnp.logical_or(p < 4, jnp.logical_not(is_first))

    def gather_to(hub):
        panel = 1 if hub else 3
        return remote(pk.at[panel], gath.at[t], hub_send.at[panel // 2], gath_recv.at[t], {"tile": hub})

    MIRRORED = (((2, 0), (5, 0)), ((2, 1), (4, 1)), ((5, 0), (2, 0)), ((4, 1), (2, 1)))

    def mirrored(n):
        (a, b), (c, d) = MIRRORED[n]
        return remote(pk.at[a, b], colh.at[c, d], mir_send.at[n], mir_recv.at[n], {"tile": mirror})

    def scatter_to(u, panel):
        return remote(scat.at[u], colh.at[panel], scat_send.at[u], scat_recv.at[panel // 2], {"tile": u})

    def seg_w(u):
        return jnp.where(is_last, LAST - u, u)

    def seg_e(u):
        return jnp.where(is_last, u, LAST - u)

    def make_scatter():
        slot = jnp.where(is_last, 16, 1)

        def one(u, c):
            for side in range(2):
                seg = seg_e(u) if side else seg_w(u)
                block, place = seg // 8, seg % 8
                out = jnp.zeros((8, 128), F32)
                for g in range(5):
                    x = field[5 - side, slot, pl.ds(8 * g, 8), pl.ds(pl.multiple_of(block * 128, 128), 128)]
                    x = pltpu.roll(x, (16 * g - 16 * place + 128) % 128, 1)
                    out = jnp.where(lanes // 16 == g, x, out)
                scat[u, side] = out

            @pl.when(jnp.logical_and(u != t, is_last))
            def _():
                scatter_to(u, 1).start()

            @pl.when(jnp.logical_and(u != t, is_first))
            def _():
                scatter_to(u, 3).start()

            return c

        lax.fori_loop(0, TILES, one, 0)

        @pl.when(is_last)
        def _():
            colh[1] = scat[t]

        @pl.when(is_first)
        def _():
            colh[3] = scat[t]

    def mix(step, c):
        p = PANELS - 1 - step
        for copy in load(p):
            copy.wait()
        xh, xl = split(xs[p].reshape(256, CELLS))
        z = dot(kz[...], jnp.concatenate([xh, xh, xl], 0))
        field[p, 1:17, 0:16, :] = z.reshape(ROWS, 16, CELLS)
        pat = ps[:, p].reshape(64, CELLS)
        q = dot(kq[...], jnp.concatenate([xh, xl, pat], 0))
        qf[p] = q.reshape(ROWS, 16, CELLS)
        wh, wl = split(ws[p].reshape(256, CELLS))
        v = dot(kv[...], jnp.concatenate([wh, wh, wl], 0))
        field[p, 1:17, 16:32, :] = v.reshape(ROWS, 16, CELLS)
        for i in range(ROWS):
            field[p, 1 + i, 32:40, :] = jnp.broadcast_to(0.5 * bs[p, i : i + 1, :], (8, CELLS))

        @pl.when(step == 0)
        def _():
            pl.semaphore_wait(barrier, TILES - 1 + SAMPS - 1)

        @pl.when(south_goes(p))
        def _():
            row_south(p).start()

        @pl.when(north_goes(p))
        def _():
            row_north(p).start()

        for side in range(2):
            if side == 0:
                rev = jnp.where(jnp.logical_or(p == 1, jnp.logical_or(p == 2, p == 5)), 1, 0)
            else:
                rev = jnp.where(jnp.logical_and(p >= 2, p <= 4), 1, 0)
            out = jnp.zeros((8, 128), F32)
            for i in range(ROWS):
                for g in range(5):
                    if side == 0:
                        x = field[p, 1 + i, 8 * g : 8 * g + 8, 0:128][:, 0:1]
                    else:
                        x = field[p, 1 + i, 8 * g : 8 * g + 8, CELLS - 128 : CELLS][:, 127:128]
                    spot = 16 * g + i + rev * (15 - 2 * i)
                    out = jnp.where(lanes == spot, jnp.broadcast_to(x, (8, 128)), out)
            pk[p, side] = out

        for at, hub in ((4, LAST), (2, 0)):
            @pl.when(jnp.logical_and(step == at, t != hub))
            def _():
                gather_to(hub).start()

            @pl.when(jnp.logical_and(step == at, t == hub))
            def _():
                gath[t] = pk[1 if hub else 3]

        @pl.when(jnp.logical_and(step == 1, is_hub))
        def _():
            make_scatter()

        @pl.when(step == 3)
        def _():
            for n in range(4):
                mirrored(n).start()

        return c

    load_p.wait()
    load_b.wait()
    lax.fori_loop(0, PANELS, mix, 0)

    colh[0, 0] = pk[5, 1]
    colh[0, 1] = pk[4, 0]
    colh[4, 0] = pk[0, 1]
    colh[5, 1] = pk[0, 0]

    first_lane, last_lane = lanes == 0, lanes == 127

    def block(g, p, slot, k):
        return field[p, slot, 8 * g : 8 * g + 8, 128 * k : 128 * k + 128]

    def stencil_row(p, i):
        slot = i + 1
        west, east = colh[p, 0], colh[p, 1]

        def sides(g):
            x = [block(g, p, slot, k) for k in range(4)]
            r = [pltpu.roll(y, 127, 1) for y in x] + [pltpu.roll(east, (127 - 16 * g - i) % 128, 1)]
            l = [pltpu.roll(west, (128 - 16 * g - i) % 128, 1)] + [pltpu.roll(y, 1, 1) for y in x]
            return (
                x,
                [jnp.where(last_lane, r[k + 1], r[k]) for k in range(4)],
                [jnp.where(first_lane, l[k], l[k + 1]) for k in range(4)],
            )

        every = [sides(g) for g in range(5)]
        for k in range(4):
            x, e, w = (v[k] for v in every[4])
            beta_e = x + e
            beta_w = x + w
            beta_s = x + block(4, p, slot + 1, k)
            beta_n = x + block(4, p, slot - 1, k)
            sums = None
            for half in range(2):
                both = []
                for g in (half, 2 + half):
                    x, e, w = (v[k] for v in every[g])
                    de = e - x
                    dw = x - w
                    ds = block(g, p, slot + 1, k) - x
                    dn = x - block(g, p, slot - 1, k)
                    lap = (beta_e * de - beta_w * dw) + (beta_s * ds - beta_n * dn)
                    both.append((lap, de, dw, ds, dn))
                (lz, *dz), (lv, *dv) = both
                q = lz + qf[p, i, 8 * half : 8 * half + 8, 128 * k : 128 * k + 128]
                terms = [x * q + y * lv for x, y in zip(dv, dz)]
                sums = terms if sums is None else [x + y for x, y in zip(sums, terms)]
            cols = slice(128 * k, 128 * k + 128)
            acc_e[p, i, :, cols] = sums[0]
            acc_w[p, i, :, cols] = sums[1]
            acc_s[p, slot + 1, :, cols] = sums[2]
            acc_n[p, slot - 1, :, cols] = sums[3]

    def stencil_rows(p, start, count):
        for r in range(count):
            stencil_row(p, start + r)

    def wait_columns():
        for n in range(4):
            mirrored(n).wait_recv()

        @pl.when(t != LAST)
        def _():
            scatter_to(LAST, 1).wait_recv()

        @pl.when(t != 0)
        def _():
            scatter_to(0, 3).wait_recv()

        turn(1, 0)
        turn(3, 1)

    def turn(p, side):
        x = colh[p, side]
        out = x
        for e in range(16):
            out = jnp.where(lanes % 16 == 15 - e, pltpu.roll(x, (15 - 2 * e) % 128, 1), out)
        colh[p, side] = out

    def inner(p, c):
        @pl.when(p == 1)
        def _():
            wait_columns()

        def seven(n, c):
            stencil_rows(p, 1 + 7 * n, 7)
            return c

        lax.fori_loop(0, 2, seven, 0)
        return c

    lax.fori_loop(0, 4, inner, 0)

    @pl.when(is_hub)
    def _():
        def wait_one(u, c):
            @pl.when(u != t)
            def _():
                remote(pk.at[1], gath.at[u], hub_send.at[0], gath_recv.at[u], {"tile": u}).wait_recv()
            return c

        lax.fori_loop(0, TILES, wait_one, 0)
        slot = jnp.where(is_last, 17, 0)

        def one(block, c):
            for side in range(2):
                for g in range(5):
                    out = jnp.zeros((8, 128), F32)
                    for k in range(8):
                        seg = 8 * block + k
                        u = seg_e(seg) if side else seg_w(seg)
                        x = pltpu.roll(gath[u, side], (16 * k - 16 * g + 128) % 128, 1)
                        out = jnp.where(lanes // 16 == k, x, out)
                    field[5 - side, slot, pl.ds(8 * g, 8), pl.ds(pl.multiple_of(block * 128, 128), 128)] = out
            return c

        lax.fori_loop(0, 4, one, 0)

    def outer(p, c):
        @pl.when(jnp.logical_or(p < 4, jnp.logical_not(is_first)))
        def _():
            came_from_left(p).wait_recv()

        @pl.when(jnp.logical_or(p < 4, jnp.logical_not(is_last)))
        def _():
            came_from_right(p).wait_recv()

        stencil_rows(p, 0, 1)
        stencil_rows(p, ROWS - 1, 1)
        return c

    lax.fori_loop(0, PANELS, outer, 0)

    def fold(matrix, x):
        high, low = split(x)
        return dot(matrix, high) + dot(matrix, low)

    fold_rows = (iota((ROWS, 8 * ROWS), 0) == iota((ROWS, 8 * ROWS), 1) // 8).astype(BF16)
    fold_panels = (iota((8, 8 * PANELS), 0) == iota((8, 8 * PANELS), 1) // 8).astype(BF16)
    lane16, row16 = iota((16, 128), 1), iota((16, 128), 0)

    prow[0] = -fold(fold_panels, acc_n[:, 0].reshape(8 * PANELS, CELLS))
    prow[1] = fold(fold_panels, acc_s[:, 17].reshape(8 * PANELS, CELLS))
    p_south = remote(prow.at[1], precv.at[0], p_send.at[0], p_recv.at[0], {"tile": right})
    p_north = remote(prow.at[0], precv.at[1], p_send.at[1], p_recv.at[1], {"tile": left})
    p_south.start()
    p_north.start()

    def fold_leaving(p, c):
        sum_e[p] = fold(fold_rows, acc_e[p].reshape(8 * ROWS, CELLS))
        sum_w[p] = fold(fold_rows, acc_w[p].reshape(8 * ROWS, CELLS))
        return c

    lax.fori_loop(0, 4, fold_leaving, 0)

    def leaving_column(p, side):
        return sum_e[p, :, CELLS - 128 :][:, 127:128] if side else -sum_w[p, :, 0:128][:, 0:1]

    def leaving_row(p, side, reverse):
        spot = 15 - row16 if reverse else row16
        column = jnp.broadcast_to(leaving_column(p, side), (16, 128))
        return jnp.sum(jnp.where(lane16 == spot, column, 0.0), axis=0, keepdims=True)

    def p_mirror(m):
        return remote(mirror_out.at[m], mirror_in.at[m], pm_send.at[m], pm_recv.at[m], {"tile": mirror})

    def send_mirror(m):
        mirror_out[m] = jnp.zeros((8, 128), F32)
        for n in range(2):
            (a, b), _ = MIRRORED[2 * m + n]
            mirror_out[m, n : n + 1, :] = leaving_row(a, b, True)
        p_mirror(m).start()

    send_mirror(0)

    def gather_p(hub):
        n = 0 if hub else 1
        return remote(hub_out.at[n], gath_p.at[t], ph_send.at[n], pgath_recv.at[t], {"tile": hub})

    up, down = t % 8, (LAST - t) % 8
    for n, hub in enumerate((LAST, 0)):
        panel = 1 if hub else 3
        hub_out[n] = jnp.zeros((8, 128), F32)
        hub_out[n, 0:1, :] = pltpu.roll(leaving_row(panel, 0, bool(hub)), 16 * (down if hub else up), 1)
        hub_out[n, 1:2, :] = pltpu.roll(leaving_row(panel, 1, not hub), 16 * (up if hub else down), 1)

        @pl.when(t != hub)
        def _():
            gather_p(hub).start()

        @pl.when(t == hub)
        def _():
            gath_p[t] = hub_out[n]

    def scatter_p(u, hub):
        n = 0 if hub else 1
        return remote(scat_p.at[u // 8], hub_in.at[n], ps_send.at[u], ps_recv.at[n], {"tile": u})

    @pl.when(is_hub)
    def _():
        rows = prow[jnp.where(is_last, 1, 0)]
        for block_at in range(4):
            ahead = rows[:, 128 * block_at : 128 * block_at + 128]
            behind = rows[:, 128 * (3 - block_at) : 128 * (3 - block_at) + 128]
            w = jnp.where(is_last, behind, ahead)
            e = jnp.where(is_last, ahead, behind)
            scat_p[block_at] = jnp.zeros((8, 128), F32)
            scat_p[block_at, 0:1, :] = w[5:6]
            scat_p[block_at, 1:2, :] = e[4:5]

        def one(u, c):
            @pl.when(jnp.logical_and(u != t, is_last))
            def _():
                scatter_p(u, LAST).start()

            @pl.when(jnp.logical_and(u != t, is_first))
            def _():
                scatter_p(u, 0).start()

            return c

        lax.fori_loop(0, TILES, one, 0)

        @pl.when(is_last)
        def _():
            hub_in[0] = scat_p[t // 8]

        @pl.when(is_first)
        def _():
            hub_in[1] = scat_p[t // 8]

    GROUPS = ((0, 1, 2, 3),)

    def each_peer(fn):
        def one(d, c):
            fn((s + d) % SAMPS)
            return c

        lax.fori_loop(1, SAMPS, one, 0)

    def reduce_to(m, peer):
        return remote(rs_in.at[m, peer], ag.at[m, s], rs_send.at[m, peer], rs_recv.at[m, s], {"samp": peer})

    def reduce_from(m, peer):
        return remote(rs_in.at[m, peer], ag.at[m, peer], rs_send.at[m, peer], rs_recv.at[m, peer], {"samp": peer})

    def share_with(m, peer):
        return remote(done.at[m, s], done.at[m, s], ag_send.at[m, peer], ag_recv.at[m, s], {"samp": peer})

    def share_from(m, peer):
        return remote(done.at[m, peer], done.at[m, peer], ag_send.at[m, peer], ag_recv.at[m, peer], {"samp": peer})

    def direct_to(peer):
        return remote(part.at[pl.ds(4, 2)], direct.at[s], rs_send.at[1, peer], rs_recv.at[1, s], {"samp": peer})

    def direct_from(peer):
        return remote(part.at[pl.ds(4, 2)], direct.at[peer], rs_send.at[1, peer], rs_recv.at[1, peer], {"samp": peer})

    def late_to(peer):
        return remote(late_in, late_ag.at[s], rs_send.at[2, peer], rs_recv.at[2, s], {"samp": peer})

    def late_from(peer):
        return remote(late_in, late_ag.at[peer], rs_send.at[2, peer], rs_recv.at[2, peer], {"samp": peer})

    def summed(parts):
        total = parts[0]
        for n in range(1, SAMPS):
            total = total + parts[n]
        return total * (0.005 / SAMPS)

    def reduce_start(m):
        for n in range(SAMPS):
            h, k = n // 4, n % 4
            for j, p in enumerate(GROUPS[m]):
                rs_in[m, n, j] = part[p, 8 * h : 8 * h + 8, 128 * k : 128 * k + 128]
        each_peer(lambda peer: reduce_to(m, peer).start())
        ag[m, s] = rs_in[m, s]

    def reduce_end(m):
        each_peer(lambda peer: reduce_from(m, peer).wait_recv())
        done[m, s] = summed([ag[m, n] for n in range(SAMPS)])
        each_peer(lambda peer: share_with(m, peer).start())

    def share_end(m):
        each_peer(lambda peer: share_from(m, peer).wait_recv())
        for n in range(SAMPS):
            h, k = n // 4, n % 4
            for j, p in enumerate(GROUPS[m]):
                out_ref[p, 8 * h : 8 * h + 8, 128 * k : 128 * k + 128] = done[m, n, j]

    cell = iota((ROWS, CELLS), 1)

    def fold_part(p, c):
        mine = (acc_s[p, 2:18] + acc_s[p, 1:17]) - (acc_n[p, 0:16] + acc_n[p, 1:17])
        to_e, to_w = sum_e[p], sum_w[p]
        moved_e = jnp.where(cell == 0, 0.0, pltpu.roll(to_e, 1, 1))
        moved_w = jnp.where(cell == CELLS - 1, 0.0, pltpu.roll(to_w, CELLS - 1, 1))
        part[p] = fold(fold_rows, mine.reshape(8 * ROWS, CELLS)) + ((to_e - to_w) + (moved_e - moved_w))
        return c

    lax.fori_loop(0, 4, fold_part, 0)
    reduce_start(0)

    lax.fori_loop(4, PANELS, inner, 0)
    sum_w[5] = fold(fold_rows, acc_w[5].reshape(8 * ROWS, CELLS))
    sum_e[4] = fold(fold_rows, acc_e[4].reshape(8 * ROWS, CELLS))
    send_mirror(1)
    sum_w[4] = fold(fold_rows, acc_w[4].reshape(8 * ROWS, CELLS))
    sum_e[5] = fold(fold_rows, acc_e[5].reshape(8 * ROWS, CELLS))
    lax.fori_loop(4, PANELS, fold_part, 0)

    def add_column(target, p, side, column):
        at, lane = (CELLS - 128, 127) if side else (0, 0)
        spread_out = jnp.broadcast_to(column, (16, 128))
        target[p, :, at : at + 128] += jnp.where(lane16 == lane, spread_out, 0.0)

    add_column(part, 5, 1, leaving_column(0, 0))
    add_column(part, 4, 0, leaving_column(0, 1))
    each_peer(lambda peer: direct_to(peer).start())
    direct[s] = part[4:6]
    reduce_end(0)

    def row_to_column(row, base, reverse):
        spot = base + (15 - row16 if reverse else row16)
        spread_out = jnp.broadcast_to(row, (16, 128))
        return jnp.sum(jnp.where(lane16 == spot, spread_out, 0.0), axis=1, keepdims=True)

    def placed(p, side, column):
        return jnp.where(lane16 == 2 * p + side, jnp.broadcast_to(column, (16, 128)), 0.0)

    p_south.wait_recv()
    p_north.wait_recv()
    from_north = precv[0]
    from_south = precv[1]
    pad = jnp.zeros((4, CELLS), F32)
    from_north = jnp.where(is_first, jnp.concatenate([from_north[3:4], from_north[0:3], pad], 0), from_north)
    from_south = jnp.where(is_last, jnp.concatenate([from_south[1:4], from_south[0:1], pad], 0), from_south)
    for n in range(SAMPS):
        h, k = n // 4, n % 4
        late_in[n] = (from_south if h else from_north)[:, 128 * k : 128 * k + 128]

    @pl.when(is_hub)
    def _():
        def wait_one(u, c):
            @pl.when(u != t)
            def _():
                remote(hub_out.at[0], gath_p.at[u], ph_send.at[0], pgath_recv.at[u], {"tile": u}).wait_recv()
            return c

        lax.fori_loop(0, TILES, wait_one, 0)
        panel_row = iota((8, 128), 0)
        first_chunk = 4 * at_end
        for block_at in range(4):
            for side in range(2):
                total = jnp.zeros((8, 128), F32)
                for k in range(8):
                    seg = 8 * block_at + k
                    total = total + gath_p[seg_e(seg) if side else seg_w(seg)]
                row = jnp.broadcast_to(total[side : side + 1, :], (8, 128))
                late_in[first_chunk + block_at] += jnp.where(panel_row == 5 - side, row, 0.0)

    @pl.when(t != LAST)
    def _():
        scatter_p(LAST, LAST).wait_recv()

    @pl.when(t != 0)
    def _():
        scatter_p(0, 0).wait_recv()

    columns = placed(0, 1, leaving_column(4, 0)) + placed(0, 0, leaving_column(5, 1))
    columns = columns + placed(1, 0, row_to_column(hub_in[0, 0:1, :], 16 * down, True))
    columns = columns + placed(1, 1, row_to_column(hub_in[0, 1:2, :], 16 * up, False))
    columns = columns + placed(3, 0, row_to_column(hub_in[1, 0:1, :], 16 * up, False))
    columns = columns + placed(3, 1, row_to_column(hub_in[1, 1:2, :], 16 * down, True))
    for m in range(2):
        p_mirror(m).wait_recv()
        for n in range(2):
            _, (a, b) = MIRRORED[2 * m + n]
            columns = columns + placed(a, b, row_to_column(mirror_in[m, n : n + 1, :], 0, False))
    late_in[8] = columns[0:8]
    late_in[9] = columns[8:16]
    each_peer(lambda peer: late_to(peer).start())
    late_ag[s] = late_in[...]
    each_peer(lambda peer: direct_from(peer).wait_recv())
    out_ref[4:6] = summed([direct[n] for n in range(SAMPS)])
    share_end(0)
    each_peer(lambda peer: late_from(peer).wait_recv())
    late_done[...] = summed([late_ag[n] for n in range(SAMPS)])
    for n in range(SAMPS):
        h, k = n // 4, n % 4
        for p in range(PANELS):
            row = slice(15, 16) if h else slice(0, 1)
            out_ref[p, row, 128 * k : 128 * k + 128] += late_done[n, p : p + 1, :]
    columns = jnp.concatenate([late_done[8], late_done[9]], 0)
    for p, side in ((0, 0), (0, 1), (1, 0), (1, 1), (3, 0), (3, 1), (2, 0), (2, 1), (5, 0), (4, 1)):
        add_column(out_ref, p, side, columns[:, 2 * p + side : 2 * p + side + 1])

    for copy_to in (lambda peer: reduce_to(0, peer), lambda peer: share_with(0, peer), direct_to, late_to):
        each_peer(lambda peer: copy_to(peer).wait_send())
    p_mirror(0).wait_send()
    p_mirror(1).wait_send()

    def rows_left(p, c):
        @pl.when(south_goes(p))
        def _():
            row_south(p).wait_send()

        @pl.when(north_goes(p))
        def _():
            row_north(p).wait_send()

        return c

    lax.fori_loop(0, PANELS, rows_left, 0)
    for n in range(4):
        mirrored(n).wait_send()
    p_south.wait_send()
    p_north.wait_send()
    for hub in (LAST, 0):
        @pl.when(t != hub)
        def _():
            gather_to(hub).wait_send()
            gather_p(hub).wait_send()

    @pl.when(is_hub)
    def _():
        def one(u, c):
            @pl.when(u != t)
            def _():
                scatter_to(u, 1).wait_send()
                scatter_p(u, LAST).wait_send()
            return c

        lax.fori_loop(0, TILES, one, 0)


def body(bathymetry, initial_state, patterns, pattern_index, coupling, final_weights):
    vmem = pl.BlockSpec(memory_space=pltpu.VMEM)
    hbm = pl.BlockSpec(memory_space=pl.ANY)
    tile = (8, 128)
    dma = pltpu.SemaphoreType.DMA
    return pl.pallas_call(
        kernel,
        out_shape=jax.ShapeDtypeStruct((PANELS, ROWS, CELLS), F32),
        in_specs=[hbm] * 6,
        out_specs=vmem,
        scratch_shapes=[
            pltpu.VMEM((1, 16), jnp.int32),
            pltpu.VMEM((16, 16), F32),
            pltpu.VMEM((PANELS, LAYERS, ROWS, CELLS), F32),
            pltpu.VMEM((PANELS, LAYERS, ROWS, CELLS), F32),
            pltpu.VMEM((4, PANELS, ROWS, CELLS), BF16),
            pltpu.VMEM((PANELS, ROWS, CELLS), F32),
            pltpu.VMEM((256, 768), BF16),
            pltpu.VMEM((256, 768), BF16),
            pltpu.VMEM((256, 576), BF16),
            pltpu.VMEM((PANELS, ROWS + 2, 40, CELLS), F32),
            pltpu.VMEM((PANELS, ROWS, LAYERS, CELLS), F32),
            pltpu.VMEM((PANELS, ROWS, 8, CELLS), F32),
            pltpu.VMEM((PANELS, ROWS, 8, CELLS), F32),
            pltpu.VMEM((PANELS, ROWS + 2, 8, CELLS), F32),
            pltpu.VMEM((PANELS, ROWS + 2, 8, CELLS), F32),
            pltpu.VMEM((PANELS, ROWS, CELLS), F32),
            pltpu.VMEM((PANELS, ROWS, CELLS), F32),
            pltpu.VMEM((PANELS, 2) + tile, F32),
            pltpu.VMEM((PANELS, 2) + tile, F32),
            pltpu.VMEM((TILES, 2) + tile, F32),
            pltpu.VMEM((TILES, 2) + tile, F32),
            pltpu.VMEM((2, 8, CELLS), F32),
            pltpu.VMEM((2, 8, CELLS), F32),
            pltpu.VMEM((2,) + tile, F32),
            pltpu.VMEM((2,) + tile, F32),
            pltpu.VMEM((2,) + tile, F32),
            pltpu.VMEM((TILES,) + tile, F32),
            pltpu.VMEM((4,) + tile, F32),
            pltpu.VMEM((2,) + tile, F32),
            pltpu.VMEM((PANELS, ROWS, CELLS), F32),
            pltpu.VMEM((1, SAMPS, 4) + tile, F32),
            pltpu.VMEM((1, SAMPS, 4) + tile, F32),
            pltpu.VMEM((1, SAMPS, 4) + tile, F32),
            pltpu.VMEM((10,) + tile, F32),
            pltpu.VMEM((SAMPS, 10) + tile, F32),
            pltpu.VMEM((10,) + tile, F32),
            pltpu.VMEM((SAMPS, 2, ROWS, CELLS), F32),
            dma((PANELS,)), dma((PANELS,)), dma((4,)),
            dma((2, PANELS)), dma((2, PANELS)),
            dma((2,)), dma((TILES,)), dma((4,)), dma((4,)),
            dma((TILES,)), dma((2,)),
            dma((2,)), dma((2,)), dma((2,)), dma((2,)),
            dma((2,)), dma((TILES,)), dma((TILES,)), dma((2,)),
            dma((3, SAMPS)), dma((3, SAMPS)), dma((1, SAMPS)), dma((1, SAMPS)),
        ],
        compiler_params=pltpu.CompilerParams(
            collective_id=0, has_side_effects=True, vmem_limit_bytes=56 * 1024 * 1024
        ),
        cost_estimate=pl.CostEstimate(flops=200_000_000, bytes_accessed=7_000_000, transcendentals=0),
    )(bathymetry, initial_state, patterns, pattern_index, coupling, final_weights)


def solution(mesh):
    in_specs = (
        P(None, "tile", None),
        P(None, None, "tile", None),
        P(None, None, "tile", None),
        P("samp", None),
        P(),
        P("samp", None, None, "tile", None),
    )
    out_specs = P(None, "tile", None)
    return jax.shard_map(body, mesh=mesh, in_specs=in_specs, out_specs=out_specs, check_vma=False)
```
